256 devices in a mesh: dp: 8 (over x, core), pencil: 32 (over y, z).
Axes of the slice: x: 4, y: 4, z: 8, core: 2. Of those that a mesh axis runs over, the one named last changes fastest.
Arguments:
- field: bfloat16 [8, 512, 512, 128], P('dp', 'pencil'), may hold values from -6 to 6
- cotangent: bfloat16 [8, 512, 512, 128], P('dp', 'pencil'), may hold values from -6 to 6
- first_core: float32 [32, 16], replicated, may hold values from -6 to 6
- second_core: float32 [16, 32, 16], P(None, 'pencil'), may hold values from -1.5 to 1.5
- output_core: float32 [16, 32, 16], replicated, may hold values from -1.5 to 1.5
- input_core: float32 [16, 32], replicated, may hold values from -1.5 to 1.5
- channel_mix: bfloat16 [32, 32], replicated, may hold values from -1 to 1
- channel_bias: float32 [32], replicated, may hold values from -3 to 3
Outputs:
- activated: bfloat16 [8, 512, 512, 128], P('dp', 'pencil')
- field_adjoint: bfloat16 [8, 512, 512, 128], P('dp', 'pencil')
- first_adjoint: float32 [32, 16], replicated
- second_adjoint: float32 [16, 32, 16], P(None, 'pencil')
- output_adjoint: float32 [16, 32, 16], replicated
- input_adjoint: float32 [16, 32], replicated
- mix_adjoint: float32 [32, 32], replicated
- bias_adjoint: float32 [32], replicated
The draws below stay inside these ranges and needn't reach their ends.
All inputs are finite; a program needn't handle non-finite values.
Results may differ from the reference program's by a relative error of at most 0.034.
Values may be sent and summed in bfloat16 or wider, within the bound.
A program may use at most 64 MiB of HBM per device.

```python
import math
import jax
import jax.numpy as jnp
from jax import lax

NX = 512
NY = 512
C = 32
MX = 32
MY = 32
RANK = 16
PLANES = 4
SAMPLES = 8
FEATS = 128


def steps_of(rng, dims, split, low, largest):
    factor_of = 1.0
    for position, parts in split:
        heights = jax.random.uniform(jax.random.fold_in(jax.random.fold_in(rng, 6), position), (parts,), jnp.float32, low / len(split), largest / len(split))
        factor_of = factor_of * jnp.repeat(jnp.exp(heights), dims[position] // parts).reshape((-1,) + (1,) * (len(dims) - 1 - position))
    return factor_of


def centred(own_key, dims, width, bound, pieces=(), kind=jnp.bfloat16):
    result = jax.random.normal(own_key, dims, jnp.float32) * width
    if len(pieces) > 0:
        result = steps_of(own_key, dims, pieces, -0.22, 0.18) * result
    return jnp.clip(result, min=-bound, max=bound).astype(kind)


def setup_inputs(seed: int = 0) -> dict:
    streams_of = jax.random.split(jax.random.key(seed), 9)
    return {
        "field": centred(streams_of[0], (SAMPLES, NX, NY, FEATS), 1.0, 6.0, ((0, 8), (1, 32))),
        "cotangent": centred(streams_of[1], (SAMPLES, NX, NY, FEATS), 1.0, 6.0, ((0, 8), (1, 32))),
        "first_core": centred(streams_of[2], (MX, RANK), 1.0, 6.0, (), jnp.float32),
        "second_core": centred(streams_of[3], (RANK, MY, RANK), RANK ** -0.5, 1.5, ((1, 32),), jnp.float32),
        "output_core": centred(streams_of[4], (RANK, C, RANK), RANK ** -0.5, 1.5, (), jnp.float32),
        "input_core": centred(streams_of[5], (RANK, C), RANK ** -0.5, 1.5, (), jnp.float32),
        "channel_mix": centred(streams_of[6], (C, C), C ** -0.5, 1.0),
        "channel_bias": centred(streams_of[7], (C,), 0.5, 3.0, (), jnp.float32),
    }


PRECISE = lax.Precision.HIGHEST

def build_second(points, retained, offset, length):
    positions = jnp.arange(length, dtype=jnp.int32) + offset
    frequency = jnp.arange(retained, dtype=jnp.int32)
    phases = positions[:, None] * frequency[None, :] % points
    angles = phases.astype(jnp.float32) * (2.0 * math.pi / points)
    factor = 1.0 / math.sqrt(points)
    stacked = jnp.stack([jnp.cos(angles) * factor, -jnp.sin(angles) * factor], axis=2)
    return stacked.reshape(length, 2 * retained).astype(jnp.bfloat16)

def build_first(points, retained, offset, length):
    positions = jnp.arange(length, dtype=jnp.int32) + offset
    frequency = jnp.arange(retained, dtype=jnp.int32)
    phases = frequency[:, None] * positions[None, :] % points
    angles = phases.astype(jnp.float32) * (2.0 * math.pi / points)
    factor = 1.0 / math.sqrt(points)
    cosine_part = jnp.cos(angles) * factor
    sine_part = jnp.sin(angles) * factor
    top_half = jnp.concatenate([cosine_part, sine_part], axis=1)
    low_half = jnp.concatenate([-sine_part, cosine_part], axis=1)
    return jnp.concatenate([top_half, low_half], axis=0).astype(jnp.bfloat16)

def mix_modes(spectrum, first_core, second_core, output_core, input_core):
    count_modes = spectrum.shape[0]
    retained = first_core.shape[0]
    channels = input_core.shape[1]
    unfolded = spectrum.reshape(count_modes, 2, retained, -1, channels)
    joined = jnp.einsum('ka,amb->mkb', first_core, second_core, precision=PRECISE)
    kernel = jnp.einsum('mkb,bdc->mkdc', joined, output_core, precision=PRECISE)
    narrowed = jnp.einsum('ci,mokpi->mokpc', input_core, unfolded, precision=PRECISE)
    widened = jnp.einsum('mkdc,mokpc->mokpd', kernel, narrowed, precision=PRECISE)
    return widened.reshape(spectrum.shape)

def activation(combined):
    cumulative = 0.5 * (1.0 + lax.erf(combined * (1.0 / math.sqrt(2.0))))
    density = jnp.exp(-0.5 * combined * combined) * (1.0 / math.sqrt(2.0 * math.pi))
    return (combined * cumulative, cumulative + combined * density)

def reference(field, cotangent, first_core, second_core, output_core, input_core, channel_mix, channel_bias):
    table_second = build_second(NY, MY, 0, NY).astype(jnp.float32)
    table_first = build_first(NX, MX, 0, NX).astype(jnp.float32)
    wide_bias = jnp.tile(channel_bias, PLANES)
    mix_wide = channel_mix.astype(jnp.float32)

    def forward_spectrum(values):
        expanded = jnp.einsum('xyf,yk->kxf', values.astype(jnp.float32), table_second, precision=PRECISE)
        stacked = expanded.astype(jnp.bfloat16).reshape(MY, 2 * NX, FEATS)
        return jnp.einsum('pq,mqf->mpf', table_first, stacked.astype(jnp.float32), precision=PRECISE)

    def inverse_spectrum(modes):
        narrow = modes.astype(jnp.bfloat16).astype(jnp.float32)
        expanded = jnp.einsum('pq,mpf->mqf', table_first, narrow, precision=PRECISE)
        stacked = expanded.astype(jnp.bfloat16).reshape(2 * MY, NX, FEATS)
        return jnp.einsum('kxf,yk->xyf', stacked.astype(jnp.float32), table_second, precision=PRECISE)

    def single_sample(sample_pair):
        source, incoming = sample_pair
        spectrum = forward_spectrum(source)
        mixed_modes, pullback = jax.vjp(mix_modes, spectrum, first_core, second_core, output_core, input_core)
        spectral = inverse_spectrum(mixed_modes)
        planar = source.astype(jnp.float32).reshape(NX, NY, PLANES, C)
        direct = jnp.einsum('xypc,cd->xypd', planar, mix_wide, precision=PRECISE).reshape(NX, NY, FEATS)
        combined = direct + spectral + wide_bias
        value, derivative = activation(combined)
        activated = value.astype(jnp.bfloat16)
        upstream = (incoming.astype(jnp.float32) * derivative).astype(jnp.bfloat16)
        upstream_modes = forward_spectrum(upstream)
        returned_modes, first_term, second_term, output_term, input_term = pullback(upstream_modes)
        returned = inverse_spectrum(returned_modes)
        planar_up = upstream.astype(jnp.float32).reshape(NX, NY, PLANES, C)
        back_direct = jnp.einsum('xypd,cd->xypc', planar_up, mix_wide, precision=PRECISE).reshape(NX, NY, FEATS)
        field_adjoint = (back_direct + returned).astype(jnp.bfloat16)
        mix_term = jnp.einsum('xypc,xypd->cd', planar, planar_up, precision=PRECISE)
        bias_term = lax.optimization_barrier(jnp.sum(planar_up, axis=(0, 1, 2)))
        return (activated, field_adjoint, first_term, second_term, output_term, input_term, mix_term, bias_term)
    results = lax.map(single_sample, (field, cotangent))
    core_scale = 1.0 / math.sqrt(SAMPLES * PLANES * MX * MY)
    mix_scale = 1.0 / math.sqrt(SAMPLES * PLANES * NX * NY)
    return (results[0], results[1], lax.optimization_barrier(jnp.sum(results[2], axis=0)) * core_scale, lax.optimization_barrier(jnp.sum(results[3], axis=0)) * core_scale, lax.optimization_barrier(jnp.sum(results[4], axis=0)) * core_scale, lax.optimization_barrier(jnp.sum(results[5], axis=0)) * core_scale, lax.optimization_barrier(jnp.sum(results[6], axis=0)) * mix_scale, lax.optimization_barrier(jnp.sum(results[7], axis=0)) * mix_scale)
```

```python
import math

import jax
import jax.numpy as jnp
import numpy as np
from jax import lax
from jax.experimental import pallas as pl
from jax.experimental.pallas import tpu as pltpu
from jax.sharding import PartitionSpec as P

F32 = jnp.float32
BF16 = jnp.bfloat16
MESH = pl.DeviceIdType.MESH
HIGHEST = lax.Precision.HIGHEST

NX = 512
NY = 512
C = 32
MX = 32
MY = 32
RANK = 16
PLANES = 4
GROUPS = 8
FEATS = 128
PENCILS = 32
ROWS = NX // PENCILS
HALF = ROWS // 2
MESSAGE = 2 * HALF
BLOCK = PENCILS * MESSAGE
CHUNK = 32
CORE_SCALE = 1.0 / math.sqrt(GROUPS * PLANES * MX * MY)
MIX_SCALE = 1.0 / math.sqrt(GROUPS * PLANES * NX * NY)


def tables():
    y = np.arange(NY, dtype=np.int64)
    m = np.arange(MY, dtype=np.int64)
    angles = (y[:, None] * m[None, :] % NY) * (2.0 * math.pi / NY)
    factor = 1.0 / math.sqrt(NY)
    second = np.stack([np.cos(angles) * factor, -np.sin(angles) * factor], axis=2).reshape(NY, 2 * MY)
    x = np.arange(NX, dtype=np.int64)
    k = np.arange(MX, dtype=np.int64)
    angles = (k[:, None] * x[None, :] % NX) * (2.0 * math.pi / NX)
    factor = 1.0 / math.sqrt(NX)
    a, b = np.cos(angles) * factor, np.sin(angles) * factor
    first = np.concatenate([np.concatenate([a, b], axis=1), np.concatenate([-b, a], axis=1)], axis=0)
    first = first.reshape(2 * MX, 2, PENCILS, 2, HALF).transpose(0, 3, 2, 1, 4).reshape(2 * MX, 2 * NX)
    second = second.astype(np.float32).astype(jnp.bfloat16)
    first = first.astype(np.float32).astype(jnp.bfloat16)
    return second, first


def dot(a, b, precision=None):
    return jnp.dot(a, b, preferred_element_type=F32, precision=precision)


def dot_nt(a, b):
    return lax.dot_general(a, b, (((1,), (1,)), ((), ())), preferred_element_type=F32)


def dot_tn(a, b, precision=None):
    return lax.dot_general(a, b, (((0,), (0,)), ((), ())), preferred_element_type=F32, precision=precision)


def iotas(shape):
    return lax.broadcasted_iota(jnp.int32, shape, 0), lax.broadcasted_iota(jnp.int32, shape, 1)


def select(shape, rule, dtype=F32):
    rows, lanes = iotas(shape)
    return jnp.where(rule(rows, lanes), 1.0, 0.0).astype(dtype)


def kernel(
    field_hbm, cot_hbm, first_core, second_core, output_core, input_core, mix, bias,
    second_t, second, first, first_t,
    act_hbm, adjoint_hbm, grads_out, second_out,
    field, cot, up, stage, scratch, sbuf, rbuf,
    joined_wide, out_wide, in_wide, mix_wide, mix_wide_t, bias_wide, narrow2, zed, spectrum, products,
    gsend, grecv, bsend, brecv, csend,
    load_sem, store_sem, ssem, rsem, gssem, grsem, bssem, brsem, cssem, crsem,
):
    me = lax.axis_index("pencil")
    group = lax.axis_index("dp")

    def load(source, target, slot, x):
        return pltpu.make_async_copy(source.at[pl.ds(x, 4)], target.at[pl.ds(x, 4)], load_sem.at[slot])

    for part in range(4):
        load(field_hbm, field, part, 4 * part).start()
    barrier = pltpu.get_barrier_semaphore()

    def greet(i, carry):
        pl.semaphore_signal(barrier, inc=1, device_id={"pencil": lax.rem(me + 1 + i, PENCILS)}, device_id_type=MESH)
        return carry

    lax.fori_loop(0, PENCILS - 1, greet, 0)

    def greet_group(i, carry):
        pl.semaphore_signal(barrier, inc=1, device_id={"dp": lax.rem(group + 1 + i, GROUPS)}, device_id_type=MESH)
        return carry

    lax.fori_loop(0, GROUPS - 1, greet_group, 0)
    for part in range(4):
        load(cot_hbm, cot, 4 + part, 4 * part).start()

    def send(turn, half):
        def start(i, carry):
            to = lax.rem(me + 1 + i, PENCILS)
            pltpu.make_async_remote_copy(
                src_ref=sbuf.at[turn, half, to],
                dst_ref=rbuf.at[turn, half, me],
                send_sem=ssem.at[turn, half],
                recv_sem=rsem.at[turn, half],
                device_id={"pencil": to},
                device_id_type=MESH,
            ).start()
            return carry

        lax.fori_loop(0, PENCILS - 1, start, 0)
        rbuf[turn, half, me] = sbuf[turn, half, me]

    def whole(turn, half):
        return pltpu.make_async_remote_copy(
            src_ref=sbuf.at[turn, half, pl.ds(0, PENCILS - 1)],
            dst_ref=rbuf.at[turn, half, pl.ds(0, PENCILS - 1)],
            send_sem=ssem.at[turn, half],
            recv_sem=rsem.at[turn, half],
            device_id={"pencil": lax.rem(me + 1, PENCILS)},
            device_id_type=MESH,
        )

    def analyse(source, x, x_half):
        pair = jnp.concatenate([source[x], source[x + 1]], axis=1)
        rows = dot(second_t[...], pair)
        scratch[pl.ds(x_half, 2 * MY, stride=HALF), :] = rows[:, :FEATS]
        scratch[pl.ds(x_half + 1, 2 * MY, stride=HALF), :] = rows[:, FEATS:]
        return rows

    def pack(turn, half):
        sbuf[turn, half] = scratch[...].astype(BF16).reshape(PENCILS, MESSAGE, FEATS)

    for half in range(2):
        for part in range(2):
            load(field_hbm, field, 2 * half + part, HALF * half + 4 * part).wait()
            for x in range(4 * part, 4 * part + 4, 2):
                analyse(field, HALF * half + x, x)
        pack(0, half)
        if half == 0:
            pl.semaphore_wait(barrier, PENCILS + GROUPS - 2)
        send(0, half)

    joined = dot(first_core[...], second_core[...], HIGHEST)
    joined2 = jnp.concatenate([joined, joined], axis=0)
    spread = select((RANK, 1024), lambda r, l: r == 2 * (l // 128) + (l % 128) // 64)
    joined_wide[...] = dot(joined2, spread, HIGHEST)
    to_pairs = select((RANK, FEATS), lambda r, l: r == l % RANK, BF16)
    out_pairs = dot(output_core[...].astype(BF16), to_pairs)
    _, lanes32 = iotas((C, FEATS))
    rows128, lanes128 = iotas((FEATS, FEATS))
    keep = (rows128 // C) == (lanes128 % 64) // RANK
    for beta in range(RANK // 2):
        low = out_pairs[2 * C * beta : 2 * C * beta + C]
        high = out_pairs[2 * C * beta + C : 2 * C * beta + 2 * C]
        one = jnp.where(lanes32 < 64, low, high)
        tiled = jnp.concatenate([one] * PLANES, axis=0)
        out_wide[:, 128 * beta : 128 * beta + 128] = jnp.where(keep, tiled, 0.0).astype(BF16)
    to_lanes = select((C, FEATS), lambda r, l: r == l % C, BF16)
    to_rows = select((FEATS, C), lambda r, l: r % C == l, BF16)
    pair_rows = select((FEATS, RANK), lambda r, l: r % RANK == l, BF16)
    in_rows = dot(pair_rows, input_core[...].astype(BF16)).astype(BF16)
    in_keep = (rows128 % 64) // RANK == lanes128 // C
    in_wide[...] = jnp.where(in_keep, dot(in_rows, to_lanes), 0.0).astype(BF16)
    same = rows128 // C == lanes128 // C
    mix_rows = dot(to_rows, mix[...]).astype(BF16)
    mix_wide[...] = jnp.where(same, dot(mix_rows, to_lanes), 0.0).astype(BF16)
    mix_rows = dot_nt(to_rows, mix[...]).astype(BF16)
    mix_wide_t[...] = jnp.where(same, dot(mix_rows, to_lanes), 0.0).astype(BF16)
    bias_wide[...] = dot(bias[...], to_lanes.astype(F32), HIGHEST)

    def gather_modes(turn):
        total = None
        for half in range(2):
            whole(turn, half).wait_recv()
            term = dot(first[:, BLOCK * half : BLOCK * (half + 1)], rbuf[turn, half].reshape(BLOCK, FEATS))
            total = term if total is None else total + term
        return total

    def scatter_modes(turn, modes):
        narrow = modes.astype(BF16)
        for half in range(2):
            rows = dot(first_t[BLOCK * half : BLOCK * (half + 1), :], narrow)
            sbuf[turn, half] = rows.astype(BF16).reshape(PENCILS, MESSAGE, FEATS)
            send(turn, half)

    modes = gather_modes(0)
    spectrum[...] = modes
    doubled = dot_nt(modes.astype(BF16), in_wide[...])
    narrow2[...] = doubled
    for beta in range(RANK // 2):
        cols = slice(128 * beta, 128 * beta + 128)
        zed[:, cols] = (joined_wide[:, cols] * doubled).astype(BF16)
    scatter_modes(1, dot_nt(zed[...], out_wide[...]))

    def unpack(turn, half):
        whole(turn, half).wait_recv()
        scratch[...] = rbuf[turn, half].astype(F32).reshape(BLOCK, FEATS)

    def store(source, target, slot, x):
        return pltpu.make_async_copy(source.at[pl.ds(x, 4)], target.at[pl.ds(x, 4)], store_sem.at[slot])

    bias_row = bias_wide[...]
    for part in range(4):
        load(cot_hbm, cot, 4 + part, 4 * part).wait()

    def activate(x, rows_x):
        rhs = jnp.concatenate([mix_wide[...], rows_x], axis=0)
        for y in range(0, NY, 128):
            lhs = jnp.concatenate([field[x, y : y + 128], second[y : y + 128]], axis=1)
            combined = dot(lhs, rhs) + bias_row
            cumulative = 0.5 + 0.5 * lax.erf(combined * math.sqrt(0.5))
            density = jnp.exp(-0.5 * combined * combined) * (1.0 / math.sqrt(2.0 * math.pi))
            stage[x, y : y + 128] = (combined * cumulative).astype(BF16)
            derivative = cumulative + combined * density
            up[x, y : y + 128] = (cot[x, y : y + 128].astype(F32) * derivative).astype(BF16)

    rows_sum = jnp.zeros((1, FEATS), F32)
    for half in range(2):
        unpack(1, half)
        base = HALF * half

        def body(j, carry, base=base):
            for s in range(2):
                x = 2 * j + s
                rows_x = scratch[pl.ds(x, 2 * MY, stride=HALF), :].astype(BF16)
                activate(base + x, rows_x)
            return carry

        lax.fori_loop(0, HALF // 2, body, 0)
        for part in range(2):
            store(stage, act_hbm, 2 * half + part, base + 4 * part).start()
        for x in range(0, HALF, 2):
            rows = analyse(up, base + x, x)
            rows_sum = rows_sum + rows[0:1, :FEATS] + rows[0:1, FEATS:]
        pack(2, half)
        send(2, half)

    products[...] = jnp.zeros_like(products)

    def accumulate(x, carry):
        products[...] += dot_tn(field[x], up[x])
        return carry

    lax.fori_loop(0, ROWS, accumulate, 0)
    folded = jnp.where(same, products[...], 0.0)
    folded = folded[0:32] + folded[32:64] + folded[64:96] + folded[96:128]
    fold_low = select((FEATS, FEATS), lambda r, l: r % C == l)
    mix_part = dot(folded, fold_low, HIGHEST)
    fold_high = select((FEATS, FEATS), lambda r, l: r % C + 64 == l)
    unit = np.float32(np.asarray(1.0 / math.sqrt(NY), dtype=np.float32).astype(jnp.bfloat16))
    bias_part = dot(rows_sum * (1.0 / float(unit)), fold_high, HIGHEST)

    upstream = gather_modes(2)
    upstream_b = upstream.astype(BF16)
    dz = dot(upstream_b, out_wide[...])
    weighted = joined_wide[...] * dz
    dn = weighted[:, 0:128]
    for beta in range(1, RANK // 2):
        dn = dn + weighted[:, 128 * beta : 128 * beta + 128]
    dn_b = dn.astype(BF16)
    scatter_modes(3, dot(dn_b, in_wide[...]))

    fold_rank = select((1024, RANK), lambda r, l: l == 2 * (r // 128) + (r % 128) // 64, BF16)
    product = jnp.concatenate(
        [dz[:, 128 * b : 128 * b + 128] * narrow2[...] for b in range(RANK // 2)], axis=1
    ).astype(BF16)
    djoined = dot(product, fold_rank)
    djoined = djoined[:MX] + djoined[MX:]
    place = select((RANK, FEATS), lambda r, l: l == r + 32)
    first_part = dot(djoined, dot_tn(second_core[...], place, HIGHEST), HIGHEST)
    second_part = dot(dot_tn(first_core[...], djoined, HIGHEST), select((RANK, FEATS), lambda r, l: l == r), HIGHEST)
    outer = dot_tn(upstream_b, zed[...])
    halves = []
    for high in range(2):
        total = None
        for low in range(4):
            beta = 4 * high + low
            block = jnp.where(keep, outer[:, 128 * beta : 128 * beta + 128], 0.0)
            block = (block[0:32] + block[32:64] + block[64:96] + block[96:128]).astype(BF16)
            fold = select(
                (FEATS, FEATS), lambda r, l, low=low: l == low * 32 + (r // 64) * RANK + r % RANK, BF16
            )
            term = dot(block, fold)
            total = term if total is None else total + term
        halves.append(total)
    inner = jnp.where(in_keep, dot_tn(dn_b, spectrum[...].astype(BF16)), 0.0)
    inner = sum(inner[RANK * i : RANK * (i + 1)] for i in range(1, 2 * PLANES)) + inner[0:RANK]
    input_part = dot(inner, fold_high, HIGHEST)
    misc = (mix_part * (MIX_SCALE / CORE_SCALE) + first_part) + jnp.concatenate(
        [input_part, bias_part * (MIX_SCALE / CORE_SCALE), jnp.zeros((15, FEATS), F32)], axis=0
    )
    for q in range(GROUPS):
        gsend[q, 0:8] = halves[q // 4][8 * (q % 4) : 8 * (q % 4) + 8]
        gsend[q, 8:12] = misc[4 * q : 4 * q + 4]
        gsend[q, 12:16] = jnp.zeros((4, FEATS), F32)
        gsend[q, 16:32] = second_part

    def start_groups(i, carry):
        to = lax.rem(group + 1 + i, GROUPS)
        pltpu.make_async_remote_copy(
            src_ref=gsend.at[to], dst_ref=grecv.at[group], send_sem=gssem, recv_sem=grsem,
            device_id={"dp": to}, device_id_type=MESH,
        ).start()
        return carry

    def all_groups(source, target, sent, received):
        return pltpu.make_async_remote_copy(
            src_ref=source, dst_ref=target, send_sem=sent, recv_sem=received,
            device_id={"dp": lax.rem(group + 1, GROUPS)}, device_id_type=MESH,
        )

    lax.fori_loop(0, GROUPS - 1, start_groups, 0)
    grecv[group] = gsend[group]
    seven = pl.ds(0, GROUPS - 1)
    all_groups(gsend.at[seven], grecv.at[seven], gssem, grsem).wait_recv()
    chunk = grecv[0]
    for q in range(1, GROUPS):
        chunk = chunk + grecv[q]
    second_out[...] = chunk[16:32] * CORE_SCALE
    bsend[...] = chunk[0:16].astype(BF16)

    def start_pencils(i, carry):
        to = lax.rem(me + 1 + i, PENCILS)
        pltpu.make_async_remote_copy(
            src_ref=bsend, dst_ref=brecv.at[me], send_sem=bssem, recv_sem=brsem,
            device_id={"pencil": to}, device_id_type=MESH,
        ).start()
        return carry

    lax.fori_loop(0, PENCILS - 1, start_pencils, 0)
    brecv[me] = bsend[...]

    def finish(x, rows_x):
        rhs = jnp.concatenate([mix_wide_t[...], rows_x], axis=0)
        for y in range(0, NY, 128):
            lhs = jnp.concatenate([up[x, y : y + 128], second[y : y + 128]], axis=1)
            cot[x, y : y + 128] = dot(lhs, rhs).astype(BF16)

    def finish_half(half):
        unpack(3, half)
        base = HALF * half

        def body(j, carry):
            for s in range(2):
                x = 2 * j + s
                rows_x = scratch[pl.ds(x, 2 * MY, stride=HALF), :].astype(BF16)
                finish(base + x, rows_x)
            return carry

        lax.fori_loop(0, HALF // 2, body, 0)
        for part in range(2):
            store(cot, adjoint_hbm, 4 + 2 * half + part, base + 4 * part).start()

    finish_half(0)
    finish_half(1)

    thirtyone = pl.ds(0, PENCILS - 1)
    pltpu.make_async_remote_copy(
        src_ref=brecv.at[thirtyone], dst_ref=brecv.at[thirtyone], send_sem=bssem, recv_sem=brsem,
        device_id={"pencil": lax.rem(me + 1, PENCILS)}, device_id_type=MESH,
    ).wait_recv()
    total = brecv[0].astype(F32)
    for q in range(1, PENCILS):
        total = total + brecv[q].astype(F32)
    csend[...] = total * CORE_SCALE

    def start_last(i, carry):
        to = lax.rem(group + 1 + i, GROUPS)
        pltpu.make_async_remote_copy(
            src_ref=csend, dst_ref=grads_out.at[group], send_sem=cssem, recv_sem=crsem,
            device_id={"dp": to}, device_id_type=MESH,
        ).start()
        return carry

    lax.fori_loop(0, GROUPS - 1, start_last, 0)
    grads_out[group] = csend[...]
    last = all_groups(grads_out.at[seven], grads_out.at[seven], cssem, crsem)
    last.wait_recv()

    last.wait_send()
    all_groups(gsend.at[seven], grecv.at[seven], gssem, grsem).wait_send()
    pltpu.make_async_remote_copy(
        src_ref=brecv.at[thirtyone], dst_ref=brecv.at[thirtyone], send_sem=bssem, recv_sem=brsem,
        device_id={"pencil": lax.rem(me + 1, PENCILS)}, device_id_type=MESH,
    ).wait_send()
    for turn in range(4):
        for half in range(2):
            whole(turn, half).wait_send()
    for part in range(4):
        store(stage, act_hbm, part, 4 * part).wait()
        store(cot, adjoint_hbm, 4 + part, 4 * part).wait()


def shards(field, cotangent, first_core, second_core, output_core, input_core, channel_mix, channel_bias):
    second, first = tables()
    slab = (ROWS, NY, FEATS)
    vmem = pl.BlockSpec(memory_space=pltpu.VMEM)
    anywhere = pl.BlockSpec(memory_space=pl.ANY)
    dma = pltpu.SemaphoreType.DMA
    act, adjoint, grads, second_total = pl.pallas_call(
        kernel,
        out_shape=[
            jax.ShapeDtypeStruct(slab, BF16),
            jax.ShapeDtypeStruct(slab, BF16),
            jax.ShapeDtypeStruct((GROUPS, 16, FEATS), F32),
            jax.ShapeDtypeStruct((16, FEATS), F32),
        ],
        in_specs=[anywhere, anywhere] + [vmem] * 10,
        out_specs=[anywhere, anywhere, vmem, vmem],
        scratch_shapes=[
            pltpu.VMEM(slab, BF16),
            pltpu.VMEM(slab, BF16),
            pltpu.VMEM(slab, BF16),
            pltpu.VMEM(slab, BF16),
            pltpu.VMEM((BLOCK, FEATS), F32),
            pltpu.VMEM((4, 2, PENCILS, MESSAGE, FEATS), BF16),
            pltpu.VMEM((4, 2, PENCILS, MESSAGE, FEATS), BF16),
            pltpu.VMEM((2 * MX, 1024), F32),
            pltpu.VMEM((FEATS, 1024), BF16),
            pltpu.VMEM((FEATS, FEATS), BF16),
            pltpu.VMEM((FEATS, FEATS), BF16),
            pltpu.VMEM((FEATS, FEATS), BF16),
            pltpu.VMEM((1, FEATS), F32),
            pltpu.VMEM((2 * MX, FEATS), F32),
            pltpu.VMEM((2 * MX, 1024), BF16),
            pltpu.VMEM((2 * MX, FEATS), F32),
            pltpu.VMEM((FEATS, FEATS), F32),
            pltpu.VMEM((GROUPS, CHUNK, FEATS), F32),
            pltpu.VMEM((GROUPS, CHUNK, FEATS), F32),
            pltpu.VMEM((16, FEATS), BF16),
            pltpu.VMEM((PENCILS, 16, FEATS), BF16),
            pltpu.VMEM((16, FEATS), F32),
            dma((8,)),
            dma((8,)),
            dma((4, 2)),
            dma((4, 2)),
            dma,
            dma,
            dma,
            dma,
            dma,
            dma,
        ],
        compiler_params=pltpu.CompilerParams(
            collective_id=0, has_side_effects=True, vmem_limit_bytes=48 * 2**20
        ),
    )(
        field[0],
        cotangent[0],
        first_core,
        second_core[:, 0, :],
        output_core.reshape(RANK * C, RANK),
        input_core,
        channel_mix,
        channel_bias[None],
        np.ascontiguousarray(second.T),
        second,
        first,
        np.ascontiguousarray(first.T),
    )
    outer = grads[:, 0:8].reshape(2, C, 8, RANK).transpose(0, 2, 1, 3).reshape(RANK, C, RANK)
    misc = grads[:, 8:12].reshape(C, FEATS)
    return (
        act[None],
        adjoint[None],
        misc[:, 32 : 32 + RANK],
        second_total[:, None, :RANK],
        outer,
        misc[:RANK, 64 : 64 + C],
        misc[:, :C],
        misc[RANK, 64 : 64 + C],
    )


def solution(mesh):
    slabs = P("dp", "pencil", None, None)
    column = P(None, "pencil", None)
    return jax.shard_map(
        shards,
        mesh=mesh,
        in_specs=(slabs, slabs, P(), column, P(), P(), P(), P()),
        out_specs=(slabs, slabs, P(), column, P(), P(), P(), P()),
        check_vma=False,
    )
```

```python
import math

import jax
import jax.numpy as jnp
import numpy as np
from jax import lax
from jax.experimental import pallas as pl
from jax.experimental.pallas import tpu as pltpu
from jax.sharding import PartitionSpec as P

F32 = jnp.float32
BF16 = jnp.bfloat16
MESH = pl.DeviceIdType.MESH
HIGHEST = lax.Precision.HIGHEST

NX = 512
NY = 512
C = 32
MX = 32
MY = 32
RANK = 16
PLANES = 4
GROUPS = 8
FEATS = 128
PENCILS = 32
ROWS = NX // PENCILS
HALF = ROWS // 2
MESSAGE = 2 * HALF
BLOCK = PENCILS * MESSAGE
CHUNK = 32
STOP = 13
CORE_SCALE = 1.0 / math.sqrt(GROUPS * PLANES * MX * MY)
MIX_SCALE = 1.0 / math.sqrt(GROUPS * PLANES * NX * NY)


def tables():
    y = np.arange(NY, dtype=np.int64)
    m = np.arange(MY, dtype=np.int64)
    angles = (y[:, None] * m[None, :] % NY) * (2.0 * math.pi / NY)
    factor = 1.0 / math.sqrt(NY)
    second = np.stack([np.cos(angles) * factor, -np.sin(angles) * factor], axis=2).reshape(NY, 2 * MY)
    x = np.arange(NX, dtype=np.int64)
    k = np.arange(MX, dtype=np.int64)
    angles = (k[:, None] * x[None, :] % NX) * (2.0 * math.pi / NX)
    factor = 1.0 / math.sqrt(NX)
    a, b = np.cos(angles) * factor, np.sin(angles) * factor
    first = np.concatenate([np.concatenate([a, b], axis=1), np.concatenate([-b, a], axis=1)], axis=0)
    first = first.reshape(2 * MX, 2, PENCILS, 2, HALF).transpose(0, 3, 2, 1, 4).reshape(2 * MX, 2 * NX)
    pad = np.zeros((NY, FEATS - 2 * MY))
    pieces = (
        [second[FEATS * i : FEATS * (i + 1)].T for i in range(NY // FEATS)]
        + [first[:, FEATS * i : FEATS * (i + 1)] for i in range(2 * NX // FEATS)]
        + [np.concatenate([second, pad], axis=1)]
        + [np.concatenate([first.T, np.concatenate([pad, pad])], axis=1)]
    )
    return np.concatenate(pieces, axis=0).astype(np.float32).astype(jnp.bfloat16)


def dot(a, b, precision=None):
    return jnp.dot(a, b, preferred_element_type=F32, precision=precision)


def dot_nt(a, b):
    return lax.dot_general(a, b, (((1,), (1,)), ((), ())), preferred_element_type=F32)


def dot_tn(a, b, precision=None):
    return lax.dot_general(a, b, (((0,), (0,)), ((), ())), preferred_element_type=F32, precision=precision)


def iotas(shape):
    return lax.broadcasted_iota(jnp.int32, shape, 0), lax.broadcasted_iota(jnp.int32, shape, 1)


def select(shape, rule, dtype=F32):
    rows, lanes = iotas(shape)
    return jnp.where(rule(rows, lanes), 1.0, 0.0).astype(dtype)


def kernel(
    field_hbm, cot_hbm, first_hbm, second_hbm, output_hbm, input_hbm, mix_hbm, bias_hbm, table_hbm,
    act, adjoint, grads_out, second_out,
    field, cot, up, scratch, sbuf, rbuf,
    first_core, second_core, output_core, input_core, mix, bias, second_t, first, second, first_t,
    joined_wide, out_wide, in_wide, mix_wide, mix_wide_t, bias_wide, narrow2, zed, spectrum, products, rows_sum,
    gsend, grecv, bsend, brecv, csend,
    load_sem, small_sem, ssem, rsem, gssem, grsem, bssem, brsem, cssem, crsem,
):
    me = lax.axis_index("pencil")
    group = lax.axis_index("dp")

    def load(source, target, slot, x):
        return pltpu.make_async_copy(source.at[pl.ds(x, 4)], target.at[pl.ds(x, 4)], load_sem.at[slot])

    smalls = []
    for i in range(NY // FEATS):
        smalls.append((table_hbm.at[pl.ds(64 * i, 64)], second_t.at[:, pl.ds(FEATS * i, FEATS)]))
    for i in range(2 * NX // FEATS):
        smalls.append((table_hbm.at[pl.ds(256 + 64 * i, 64)], first.at[:, pl.ds(FEATS * i, FEATS)]))
    smalls.append((table_hbm.at[pl.ds(768, NY)], second))
    smalls.append((table_hbm.at[pl.ds(768 + NY, 2 * NX)], first_t))
    smalls += [
        (first_hbm, first_core), (second_hbm, second_core), (output_hbm, output_core),
        (input_hbm, input_core), (mix_hbm, mix), (bias_hbm, bias),
    ]
    copies = [pltpu.make_async_copy(a, b, small_sem.at[i]) for i, (a, b) in enumerate(smalls)]

    for copy in copies[:4]:
        copy.start()
    load(field_hbm, field, 0, 0).start()
    barrier = pltpu.get_barrier_semaphore()

    def greet(i, carry):
        pl.semaphore_signal(barrier, inc=1, device_id={"pencil": lax.rem(me + 1 + i, PENCILS)}, device_id_type=MESH)
        return carry

    lax.fori_loop(0, PENCILS - 1, greet, 0)

    def greet_group(i, carry):
        pl.semaphore_signal(barrier, inc=1, device_id={"dp": lax.rem(group + 1 + i, GROUPS)}, device_id_type=MESH)
        return carry

    lax.fori_loop(0, GROUPS - 1, greet_group, 0)
    for part in range(1, 4):
        load(field_hbm, field, part, 4 * part).start()
    for copy in copies[4:]:
        copy.start()
    for part in range(4):
        load(cot_hbm, cot, 4 + part, 4 * part).start()

    def send(turn, half):
        def start(i, carry):
            to = lax.rem(me + 1 + i, PENCILS)
            pltpu.make_async_remote_copy(
                src_ref=sbuf.at[turn, half, to],
                dst_ref=rbuf.at[turn, half, me],
                send_sem=ssem.at[turn, half],
                recv_sem=rsem.at[turn, half],
                device_id={"pencil": to},
                device_id_type=MESH,
            ).start()
            return carry

        lax.fori_loop(0, PENCILS - 1, start, 0)
        rbuf[turn, half, me] = sbuf[turn, half, me]

    def whole(turn, half):
        return pltpu.make_async_remote_copy(
            src_ref=sbuf.at[turn, half, pl.ds(0, PENCILS - 1)],
            dst_ref=rbuf.at[turn, half, pl.ds(0, PENCILS - 1)],
            send_sem=ssem.at[turn, half],
            recv_sem=rsem.at[turn, half],
            device_id={"pencil": lax.rem(me + 1, PENCILS)},
            device_id_type=MESH,
        )

    def analyse(source, x, x_half):
        pair = jnp.concatenate([source[x], source[x + 1]], axis=1)
        rows = dot(second_t[...], pair)
        scratch[pl.ds(x_half, 2 * MY, stride=HALF), :] = rows[:, :FEATS]
        scratch[pl.ds(x_half + 1, 2 * MY, stride=HALF), :] = rows[:, FEATS:]
        return rows

    def pack(turn, half):
        sbuf[turn, half] = scratch[...].astype(BF16).reshape(PENCILS, MESSAGE, FEATS)

    def gather_modes(turn):
        total = None
        for half in range(2):
            whole(turn, half).wait_recv()
            term = dot(first[:, BLOCK * half : BLOCK * (half + 1)], rbuf[turn, half].reshape(BLOCK, FEATS))
            total = term if total is None else total + term
        return total

    def scatter_modes(turn, modes):
        narrow = modes.astype(BF16)
        for half in range(2):
            rows = dot(first_t[BLOCK * half : BLOCK * (half + 1), : 2 * MX], narrow)
            sbuf[turn, half] = rows.astype(BF16).reshape(PENCILS, MESSAGE, FEATS)
            send(turn, half)

    def unpack(turn, half):
        whole(turn, half).wait_recv()
        scratch[...] = rbuf[turn, half].astype(F32).reshape(BLOCK, FEATS)

    rows128, lanes128 = iotas((FEATS, FEATS))
    same = rows128 // C == lanes128 // C
    in_keep = (rows128 % 64) // RANK == lanes128 // C

    def field_rows():
        for copy in copies[:4]:
            copy.wait()
        for half in range(2):
            for part in range(2):
                load(field_hbm, field, 2 * half + part, HALF * half + 4 * part).wait()
                for x in range(4 * part, 4 * part + 4, 2):
                    analyse(field, HALF * half + x, x)
            pack(0, half)
            if half == 0:
                pl.semaphore_wait(barrier, PENCILS + GROUPS - 2)
            send(0, half)

    def weights():
        for copy in copies[4:]:
            copy.wait()
        joined = dot_tn(first_core[...], second_core[...], HIGHEST)
        joined2 = jnp.concatenate([joined, joined], axis=0)
        spread = select((RANK, 1024), lambda r, l: r == 2 * (l // 128) + (l % 128) // 64)
        joined_wide[...] = dot(joined2, spread, HIGHEST)
        to_lanes = select((C, FEATS), lambda r, l: r == l % C, BF16)
        to_rows = select((FEATS, C), lambda r, l: r % C == l, BF16)
        pair_rows = select((FEATS, RANK), lambda r, l: r % RANK == l, BF16)
        for beta in range(RANK // 2):
            rows = output_core[2 * RANK * beta : 2 * RANK * beta + 2 * RANK].astype(BF16)
            low, high = rows[:RANK], rows[RANK:]
            tall = jnp.concatenate([low] * PLANES + [high] * PLANES, axis=0)
            wide = jnp.where(in_keep, dot(tall, to_lanes), 0.0)
            out_wide[128 * beta : 128 * beta + 128, :] = wide.astype(BF16)
        in_rows = dot(pair_rows, input_core[...].astype(BF16)).astype(BF16)
        in_wide[...] = jnp.where(in_keep, dot(in_rows, to_lanes), 0.0).astype(BF16)
        mix_rows = dot(to_rows, mix[...]).astype(BF16)
        mix_wide[...] = jnp.where(same, dot(mix_rows, to_lanes), 0.0).astype(BF16)
        mix_rows = dot_nt(to_rows, mix[...]).astype(BF16)
        mix_wide_t[...] = jnp.where(same, dot(mix_rows, to_lanes), 0.0).astype(BF16)
        bias_wide[...] = dot(bias[...], to_lanes.astype(F32), HIGHEST)
        for part in range(4):
            load(cot_hbm, cot, 4 + part, 4 * part).wait()

    def mix_forward():
        modes = gather_modes(0)
        spectrum[...] = modes
        doubled = dot_nt(modes.astype(BF16), in_wide[...])
        narrow2[...] = doubled
        for beta in range(RANK // 2):
            cols = slice(128 * beta, 128 * beta + 128)
            zed[:, cols] = (joined_wide[:, cols] * doubled).astype(BF16)
        scatter_modes(1, dot(zed[...], out_wide[...]))

    def activate(x, rows_x):
        rhs = jnp.concatenate([mix_wide[...], rows_x], axis=0)
        for y in range(0, NY, 128):
            lhs = jnp.concatenate([field[x, y : y + 128], second[y : y + 128, : 2 * MY]], axis=1)
            combined = dot(lhs, rhs) + bias_wide[...]
            cumulative = 0.5 + 0.5 * lax.erf(combined * math.sqrt(0.5))
            density = jnp.exp(-0.5 * combined * combined) * (1.0 / math.sqrt(2.0 * math.pi))
            act[x, y : y + 128] = (combined * cumulative).astype(BF16)
            derivative = cumulative + combined * density
            up[x, y : y + 128] = (cot[x, y : y + 128].astype(F32) * derivative).astype(BF16)

    def sweep(base, step):
        def body(j, carry):
            for s in range(2):
                x = 2 * j + s
                step(base + x, scratch[pl.ds(x, 2 * MY, stride=HALF), :].astype(BF16))
            return carry

        lax.fori_loop(0, HALF // 2, body, 0)

    def activation():
        total = jnp.zeros((1, FEATS), F32)
        for half in range(2):
            unpack(1, half)
            base = HALF * half
            sweep(base, activate)
            for x in range(0, HALF, 2):
                rows = analyse(up, base + x, x)
                total = total + rows[0:1, :FEATS] + rows[0:1, FEATS:]
            pack(2, half)
            send(2, half)
        rows_sum[...] = total

    def mix_gradient():
        products[...] = jnp.zeros_like(products)

        def accumulate(x, carry):
            products[...] += dot_tn(field[x], up[x])
            return carry

        lax.fori_loop(0, ROWS, accumulate, 0)

    def mix_backward():
        upstream = gather_modes(2)
        upstream_b = upstream.astype(BF16)
        dz = dot_nt(upstream_b, out_wide[...])
        dn = joined_wide[:, 0:128] * dz[:, 0:128]
        for beta in range(1, RANK // 2):
            cols = slice(128 * beta, 128 * beta + 128)
            dn = dn + joined_wide[:, cols] * dz[:, cols]
        dn_b = dn.astype(BF16)
        scatter_modes(3, dot(dn_b, in_wide[...]))
        return upstream_b, dz, dn_b

    def core_gradients(upstream_b, dz, dn_b):
        product = jnp.concatenate(
            [dz[:, 128 * b : 128 * b + 128] * narrow2[...] for b in range(RANK // 2)], axis=1
        ).astype(BF16)
        fold_rank = select((1024, RANK), lambda r, l: l == 2 * (r // 128) + (r % 128) // 64, BF16)
        djoined = dot(product, fold_rank)
        djoined = djoined[:MX] + djoined[MX:]
        place = select((MX, FEATS), lambda r, l: l == r + 32)
        first_part = dot(lax.dot_general(second_core[...], djoined, (((1,), (1,)), ((), ())), precision=HIGHEST), place, HIGHEST)
        unit = select((RANK, FEATS), lambda r, l: l == r)
        second_part = dot(dot(first_core[...], djoined, HIGHEST), unit, HIGHEST)
        packed = None
        for quarter in range(4):
            rows = []
            for beta in (2 * quarter, 2 * quarter + 1):
                outer = dot_tn(zed[:, 128 * beta : 128 * beta + 128], upstream_b)
                outer = jnp.where(in_keep, outer, 0.0)
                for base in (0, 64):
                    rows.append(
                        (outer[base : base + 16] + outer[base + 16 : base + 32])
                        + (outer[base + 32 : base + 48] + outer[base + 48 : base + 64])
                    )
            fold = select((FEATS, FEATS), lambda r, l, q=quarter: r % C + 32 * q == l, BF16)
            term = dot(jnp.concatenate(rows, axis=0).astype(BF16), fold)
            packed = term if packed is None else packed + term
        inner = jnp.where(in_keep, dot_tn(dn_b, spectrum[...].astype(BF16)), 0.0)
        inner = sum(inner[RANK * i : RANK * (i + 1)] for i in range(1, 2 * PLANES)) + inner[0:RANK]
        mixed = jnp.where(same, products[...], 0.0) * (MIX_SCALE / CORE_SCALE)
        mixed = (mixed[0:32] + mixed[32:64]) + (mixed[64:96] + mixed[96:128])
        stacked = jnp.concatenate([inner, mixed[:RANK], mixed[RANK:]], axis=1)
        fold = select(
            (3 * FEATS, FEATS), lambda r, l: r % C + jnp.where(r < FEATS, 0, 32 + 32 * (r // FEATS)) == l
        )
        misc = dot(stacked, fold, HIGHEST) + first_part
        unit = float(np.asarray(1.0 / math.sqrt(NY), dtype=np.float32).astype(jnp.bfloat16))
        bias_part = rows_sum[...] * (MIX_SCALE / CORE_SCALE / unit)
        for q in range(GROUPS):
            gsend[q, 0:8] = packed[8 * q : 8 * q + 8]
            gsend[q, 8:10] = misc[2 * q : 2 * q + 2]
            gsend[q, 10:11] = bias_part
            gsend[q, 11:16] = jnp.zeros((5, FEATS), F32)
            gsend[q, 16:32] = second_part

    def to_groups(source, target, sent, received):
        def start(i, carry):
            to = lax.rem(group + 1 + i, GROUPS)
            pltpu.make_async_remote_copy(
                src_ref=source(to), dst_ref=target.at[group], send_sem=sent, recv_sem=received,
                device_id={"dp": to}, device_id_type=MESH,
            ).start()
            return carry

        lax.fori_loop(0, GROUPS - 1, start, 0)

    def all_groups(target, sent, received):
        seven = target.at[pl.ds(0, GROUPS - 1)]
        return pltpu.make_async_remote_copy(
            src_ref=seven, dst_ref=seven, send_sem=sent, recv_sem=received,
            device_id={"dp": lax.rem(group + 1, GROUPS)}, device_id_type=MESH,
        )

    def all_pencils():
        others = brecv.at[pl.ds(0, PENCILS - 1)]
        return pltpu.make_async_remote_copy(
            src_ref=others, dst_ref=others, send_sem=bssem, recv_sem=brsem,
            device_id={"pencil": lax.rem(me + 1, PENCILS)}, device_id_type=MESH,
        )

    def sum_groups_send():
        to_groups(lambda to: gsend.at[to], grecv, gssem, grsem)
        grecv[group] = gsend[group]

    def sum_groups():
        all_groups(grecv, gssem, grsem).wait_recv()
        chunk = grecv[0]
        for q in range(1, GROUPS):
            chunk = chunk + grecv[q]
        second_out[...] = chunk[16:32] * CORE_SCALE
        bsend[...] = chunk[0:16].astype(BF16)

        def start(i, carry):
            to = lax.rem(me + 1 + i, PENCILS)
            pltpu.make_async_remote_copy(
                src_ref=bsend, dst_ref=brecv.at[me], send_sem=bssem, recv_sem=brsem,
                device_id={"pencil": to}, device_id_type=MESH,
            ).start()
            return carry

        lax.fori_loop(0, PENCILS - 1, start, 0)
        brecv[me] = bsend[...]

    def finish(x, rows_x):
        rhs = jnp.concatenate([mix_wide_t[...], rows_x], axis=0)
        for y in range(0, NY, 128):
            lhs = jnp.concatenate([up[x, y : y + 128], second[y : y + 128, : 2 * MY]], axis=1)
            adjoint[x, y : y + 128] = dot(lhs, rhs).astype(BF16)

    def finish_half(half):
        unpack(3, half)
        sweep(HALF * half, finish)

    def sum_pencils():
        all_pencils().wait_recv()
        total = brecv[0].astype(F32)
        for q in range(1, PENCILS):
            total = total + brecv[q].astype(F32)
        csend[...] = total * CORE_SCALE
        to_groups(lambda to: csend, grads_out, cssem, crsem)
        grads_out[group] = csend[...]

    def last():
        all_groups(grads_out, cssem, crsem).wait_recv()

    state = {}
    steps = [
        field_rows, weights, mix_forward, activation, mix_gradient,
        lambda: state.update(modes=mix_backward()),
        lambda: core_gradients(*state["modes"]),
        sum_groups_send, sum_groups, lambda: finish_half(0), lambda: finish_half(1), sum_pencils, last,
    ]
    for step in steps[:STOP]:
        step()

    if STOP > 12:
        all_groups(grads_out, cssem, crsem).wait_send()
    if STOP > 7:
        all_groups(grecv, gssem, grsem).wait_send()
    if STOP > 8:
        all_pencils().wait_send()
    for turn in range(4 if STOP > 5 else 3 if STOP > 3 else 2 if STOP > 2 else 1):
        for half in range(2):
            whole(turn, half).wait_send()


def write_out(
    act, adjoint, grads, second_in,
    act_hbm, adjoint_hbm, first_hbm, second_hbm, output_hbm, input_hbm, mix_hbm, bias_hbm,
    first, second, output, inner, mix, bias, sem,
):
    large = [
        pltpu.make_async_copy(act, act_hbm, sem.at[0]),
        pltpu.make_async_copy(adjoint, adjoint_hbm, sem.at[1]),
    ]
    for copy in large:
        copy.start()
    second[...] = second_in[:, :RANK]
    packed = grads[:, 0:8].reshape(64, FEATS)
    for quarter in range(4):
        output[64 * quarter : 64 * quarter + 64] = packed[:, 32 * quarter : 32 * quarter + 32]
    misc = jnp.concatenate([grads[q, 8:10] for q in range(GROUPS)], axis=0)
    inner[...] = misc[:, 0:32]
    first[...] = misc[:, 32:64]
    mix[0:RANK] = misc[:, 64:96]
    mix[RANK:C] = misc[:, 96:128]
    row = grads[0, 10:11]
    bias[...] = (row[:, 0:32] + row[:, 32:64]) + (row[:, 64:96] + row[:, 96:128])
    pairs = [
        (first, first_hbm), (second, second_hbm), (output, output_hbm),
        (inner, input_hbm), (mix, mix_hbm), (bias, bias_hbm),
    ]
    small = [pltpu.make_async_copy(a, b, sem.at[2 + i]) for i, (a, b) in enumerate(pairs)]
    for copy in small:
        copy.start()
    for copy in large + small:
        copy.wait()


def shards(field, cotangent, first_core, second_core, output_core, input_core, channel_mix, channel_bias):
    slab = (ROWS, NY, FEATS)
    vmem = pl.BlockSpec(memory_space=pltpu.VMEM)
    hbm = pl.BlockSpec(memory_space=pltpu.HBM)
    dma = pltpu.SemaphoreType.DMA
    smalls = [(RANK, MX), (RANK, RANK), (RANK * RANK, C), (RANK, C), (C, C), (1, C)]
    types = [F32, F32, F32, F32, BF16, F32]
    act, adjoint, grads, second_total = pl.pallas_call(
        kernel,
        out_shape=[
            jax.ShapeDtypeStruct(slab, BF16),
            jax.ShapeDtypeStruct(slab, BF16),
            jax.ShapeDtypeStruct((GROUPS, 16, FEATS), F32),
            jax.ShapeDtypeStruct((16, FEATS), F32),
        ],
        in_specs=[hbm] * 9,
        out_specs=[vmem] * 4,
        scratch_shapes=[
            pltpu.VMEM(slab, BF16),
            pltpu.VMEM(slab, BF16),
            pltpu.VMEM(slab, BF16),
            pltpu.VMEM((BLOCK, FEATS), F32),
            pltpu.VMEM((4, 2, PENCILS, MESSAGE, FEATS), BF16),
            pltpu.VMEM((4, 2, PENCILS, MESSAGE, FEATS), BF16),
        ]
        + [pltpu.VMEM(s, t) for s, t in zip(smalls, types)]
        + [
            pltpu.VMEM((2 * MY, NY), BF16),
            pltpu.VMEM((2 * MX, 2 * NX), BF16),
            pltpu.VMEM((NY, FEATS), BF16),
            pltpu.VMEM((2 * NX, FEATS), BF16),
            pltpu.VMEM((2 * MX, 1024), F32),
            pltpu.VMEM((1024, FEATS), BF16),
            pltpu.VMEM((FEATS, FEATS), BF16),
            pltpu.VMEM((FEATS, FEATS), BF16),
            pltpu.VMEM((FEATS, FEATS), BF16),
            pltpu.VMEM((1, FEATS), F32),
            pltpu.VMEM((2 * MX, FEATS), F32),
            pltpu.VMEM((2 * MX, 1024), BF16),
            pltpu.VMEM((2 * MX, FEATS), F32),
            pltpu.VMEM((FEATS, FEATS), F32),
            pltpu.VMEM((1, FEATS), F32),
            pltpu.VMEM((GROUPS, CHUNK, FEATS), F32),
            pltpu.VMEM((GROUPS, CHUNK, FEATS), F32),
            pltpu.VMEM((16, FEATS), BF16),
            pltpu.VMEM((PENCILS, 16, FEATS), BF16),
            pltpu.VMEM((16, FEATS), F32),
            dma((8,)),
            dma((20,)),
            dma((4, 2)),
            dma((4, 2)),
            dma,
            dma,
            dma,
            dma,
            dma,
            dma,
        ],
        compiler_params=pltpu.CompilerParams(
            collective_id=0, has_side_effects=True, vmem_limit_bytes=40 * 2**20
        ),
    )(
        *[
            pltpu.with_memory_space_constraint(a, pltpu.HBM)
            for a in (
                field[0],
                cotangent[0],
                first_core.T,
                second_core[:, 0, :],
                output_core.transpose(0, 2, 1).reshape(RANK * RANK, C),
                input_core,
                channel_mix,
                channel_bias[None],
                jnp.asarray(tables()),
            )
        ]
    )
    results = pl.pallas_call(
        write_out,
        out_shape=[jax.ShapeDtypeStruct(slab, BF16), jax.ShapeDtypeStruct(slab, BF16)]
        + [jax.ShapeDtypeStruct(s, F32) for s in smalls],
        in_specs=[vmem] * 4,
        out_specs=[hbm] * 8,
        scratch_shapes=[pltpu.VMEM(s, F32) for s in smalls] + [dma((8,))],
        compiler_params=pltpu.CompilerParams(vmem_limit_bytes=16 * 2**20),
    )(act, adjoint, grads, second_total)
    act, adjoint, first, second, output, inner, mix, bias = results
    return (
        act[None],
        adjoint[None],
        first.T,
        second[:, None, :],
        output.reshape(RANK, RANK, C).transpose(0, 2, 1),
        inner,
        mix,
        bias[0],
    )


def solution(mesh):
    slabs = P("dp", "pencil", None, None)
    column = P(None, "pencil", None)
    return jax.shard_map(
        shards,
        mesh=mesh,
        in_specs=(slabs, slabs, P(), column, P(), P(), P(), P()),
        out_specs=(slabs, slabs, P(), column, P(), P(), P(), P()),
        check_vma=False,
    )
```

```python
import math

import jax
import jax.numpy as jnp
import numpy as np
from jax import lax
from jax.experimental import pallas as pl
from jax.experimental.pallas import tpu as pltpu
from jax.sharding import PartitionSpec as P

F32 = jnp.float32
BF16 = jnp.bfloat16
MESH = pl.DeviceIdType.MESH
HIGHEST = lax.Precision.HIGHEST

NX = 512
NY = 512
C = 32
MX = 32
MY = 32
RANK = 16
PLANES = 4
GROUPS = 8
FEATS = 128
PENCILS = 32
ROWS = NX // PENCILS
HALF = ROWS // 2
MESSAGE = 2 * HALF
BLOCK = PENCILS * MESSAGE
YS, ZS = 4, 8
PARTS = GROUPS * YS
CHUNK = 4
STOP = 15
CORE_SCALE = 1.0 / math.sqrt(GROUPS * PLANES * MX * MY)
MIX_SCALE = 1.0 / math.sqrt(GROUPS * PLANES * NX * NY)


def tables():
    y = np.arange(NY, dtype=np.int64)
    m = np.arange(MY, dtype=np.int64)
    angles = (y[:, None] * m[None, :] % NY) * (2.0 * math.pi / NY)
    factor = 1.0 / math.sqrt(NY)
    second = np.stack([np.cos(angles) * factor, -np.sin(angles) * factor], axis=2).reshape(NY, 2 * MY)
    x = np.arange(NX, dtype=np.int64)
    k = np.arange(MX, dtype=np.int64)
    angles = (k[:, None] * x[None, :] % NX) * (2.0 * math.pi / NX)
    factor = 1.0 / math.sqrt(NX)
    a, b = np.cos(angles) * factor, np.sin(angles) * factor
    first = np.concatenate([np.concatenate([a, b], axis=1), np.concatenate([-b, a], axis=1)], axis=0)
    first = first.reshape(2 * MX, 2, PENCILS, 2, HALF).transpose(0, 3, 2, 1, 4).reshape(2 * MX, 2 * NX)
    pad = np.zeros((NY, FEATS - 2 * MY))
    pieces = (
        [second[FEATS * i : FEATS * (i + 1)].T for i in range(NY // FEATS)]
        + [first[:, FEATS * i : FEATS * (i + 1)] for i in range(2 * NX // FEATS)]
        + [np.concatenate([second, pad], axis=1)]
        + [np.concatenate([first.T, np.concatenate([pad, pad])], axis=1)]
    )
    return np.concatenate(pieces, axis=0).astype(np.float32).astype(jnp.bfloat16)


def dot(a, b, precision=None):
    return jnp.dot(a, b, preferred_element_type=F32, precision=precision)


def dot_nt(a, b):
    return lax.dot_general(a, b, (((1,), (1,)), ((), ())), preferred_element_type=F32)


def dot_tn(a, b, precision=None):
    return lax.dot_general(a, b, (((0,), (0,)), ((), ())), preferred_element_type=F32, precision=precision)


def iotas(shape):
    return lax.broadcasted_iota(jnp.int32, shape, 0), lax.broadcasted_iota(jnp.int32, shape, 1)


def select(shape, rule, dtype=F32):
    rows, lanes = iotas(shape)
    return jnp.where(rule(rows, lanes), 1.0, 0.0).astype(dtype)


def kernel(
    field_hbm, cot_hbm, first_hbm, second_hbm, output_hbm, input_hbm, mix_hbm, bias_hbm, table_hbm,
    act, adjoint, grads_out, second_out,
    field, cot, up, scratch, analysed, sbuf, rbuf,
    first_core, second_core, output_core, input_core, mix, bias, second_t, first, second, first_t,
    joined_wide, out_wide, in_wide, mix_wide, mix_wide_t, bias_wide, narrow2, zed, spectrum, products, rows_sum, fold_rank, fold_lanes, misc,
    gsend, grecv, bsend, brecv, csend, hsend, hrecv,
    load_sem, small_sem, ssem, rsem, gssem, grsem, bssem, brsem, cssem, crsem, hssem, hrsem,
):
    me = lax.axis_index("pencil")
    group = lax.axis_index("dp")
    z = lax.rem(me, ZS)
    mine = group * YS + lax.div(me, ZS)

    def load(source, target, slot, x):
        return pltpu.make_async_copy(source.at[pl.ds(x, 4)], target.at[pl.ds(x, 4)], load_sem.at[slot])

    smalls = []
    for i in range(NY // FEATS):
        smalls.append((table_hbm.at[pl.ds(64 * i, 64)], second_t.at[:, pl.ds(FEATS * i, FEATS)]))
    for i in range(2 * NX // FEATS):
        smalls.append((table_hbm.at[pl.ds(256 + 64 * i, 64)], first.at[:, pl.ds(FEATS * i, FEATS)]))
    smalls.append((table_hbm.at[pl.ds(768, NY)], second))
    smalls.append((table_hbm.at[pl.ds(768 + NY, 2 * NX)], first_t))
    smalls += [
        (first_hbm, first_core), (second_hbm, second_core), (output_hbm, output_core),
        (input_hbm, input_core), (mix_hbm, mix), (bias_hbm, bias),
    ]
    copies = [pltpu.make_async_copy(a, b, small_sem.at[i]) for i, (a, b) in enumerate(smalls)]

    for copy in copies[:4]:
        copy.start()
    load(field_hbm, field, 0, 0).start()
    barrier = pltpu.get_barrier_semaphore()

    def wrap(i, size):
        return jnp.where(i >= size, i - size, i)

    column = me - z
    greeted = [{"pencil": wrap(me + i, PENCILS)} for i in range(1, PENCILS)]
    for i in range(1, GROUPS):
        to = wrap(group + i, GROUPS)
        greeted += [{"dp": to, "pencil": y * ZS + z} for y in range(YS)]
    for to in greeted:
        pl.semaphore_signal(barrier, inc=1, device_id=to, device_id_type=MESH)
    for part in range(1, 4):
        load(field_hbm, field, part, 4 * part).start()
    for copy in copies[4:]:
        copy.start()
    for part in range(4):
        load(cot_hbm, cot, 4 + part, 4 * part).start()

    def send(turn, half):
        def start(i, carry):
            to = wrap(me + 1 + i, PENCILS)
            pltpu.make_async_remote_copy(
                src_ref=sbuf.at[turn, half, to],
                dst_ref=rbuf.at[turn, half, me],
                send_sem=ssem.at[turn, half],
                recv_sem=rsem.at[turn, half],
                device_id={"pencil": to},
                device_id_type=MESH,
            ).start()
            return carry

        lax.fori_loop(0, PENCILS - 1, start, 0, unroll=4)
        rbuf[turn, half, me] = sbuf[turn, half, me]

    def whole(turn, half):
        return pltpu.make_async_remote_copy(
            src_ref=sbuf.at[turn, half, pl.ds(0, PENCILS - 1)],
            dst_ref=rbuf.at[turn, half, pl.ds(0, PENCILS - 1)],
            send_sem=ssem.at[turn, half],
            recv_sem=rsem.at[turn, half],
            device_id={"pencil": lax.rem(me + 1, PENCILS)},
            device_id_type=MESH,
        )

    def analyse(source, x, x_half):
        pair = jnp.concatenate([source[x], source[x + 1]], axis=1)
        rows = dot(second_t[...], pair)
        analysed[pl.ds(x_half, 2 * MY, stride=HALF), :] = rows[:, :FEATS]
        analysed[pl.ds(x_half + 1, 2 * MY, stride=HALF), :] = rows[:, FEATS:]
        return rows

    def pack(turn, half):
        sbuf[turn, half] = analysed[...].astype(BF16).reshape(PENCILS, MESSAGE, FEATS)

    def gather_modes(turn):
        total = None
        for half in range(2):
            whole(turn, half).wait_recv()
            term = dot(first[:, BLOCK * half : BLOCK * (half + 1)], rbuf[turn, half].reshape(BLOCK, FEATS))
            total = term if total is None else total + term
        return total

    def scatter_modes(turn, modes):
        narrow = modes.astype(BF16)
        for half in range(2):
            rows = dot(first_t[BLOCK * half : BLOCK * (half + 1), : 2 * MX], narrow)
            sbuf[turn, half] = rows.astype(BF16).reshape(PENCILS, MESSAGE, FEATS)
            send(turn, half)

    def unpack(turn, half):
        whole(turn, half).wait_recv()
        scratch[...] = rbuf[turn, half].astype(F32).reshape(BLOCK, FEATS)

    rows128, lanes128 = iotas((FEATS, FEATS))
    same = rows128 // C == lanes128 // C
    in_keep = (rows128 % 64) // RANK == lanes128 // C

    def field_rows():
        for copy in copies[:4]:
            copy.wait()
        for half in range(2):
            for part in range(2):
                load(field_hbm, field, 2 * half + part, HALF * half + 4 * part).wait()
                for x in range(4 * part, 4 * part + 4, 2):
                    analyse(field, HALF * half + x, x)
            pack(0, half)
        pl.semaphore_wait(barrier, len(greeted))
        for half in range(2):
            send(0, half)

    def weights():
        for copy in copies[4:]:
            copy.wait()
        joined = dot_tn(first_core[...], second_core[...], HIGHEST)
        joined2 = jnp.concatenate([joined, joined], axis=0)
        spread = select((RANK, 1024), lambda r, l: r == 2 * (l // 128) + (l % 128) // 64)
        joined_wide[...] = dot(joined2, spread, HIGHEST)
        to_lanes = select((C, FEATS), lambda r, l: r == l % C, BF16)
        to_rows = select((FEATS, C), lambda r, l: r % C == l, BF16)
        pair_rows = select((FEATS, RANK), lambda r, l: r % RANK == l, BF16)
        for beta in range(RANK // 2):
            rows = output_core[2 * RANK * beta : 2 * RANK * beta + 2 * RANK].astype(BF16)
            low, high = rows[:RANK], rows[RANK:]
            tall = jnp.concatenate([low] * PLANES + [high] * PLANES, axis=0)
            wide = jnp.where(in_keep, dot(tall, to_lanes), 0.0)
            out_wide[128 * beta : 128 * beta + 128, :] = wide.astype(BF16)
        in_rows = dot(pair_rows, input_core[...].astype(BF16)).astype(BF16)
        in_wide[...] = jnp.where(in_keep, dot(in_rows, to_lanes), 0.0).astype(BF16)
        mix_rows = dot(to_rows, mix[...]).astype(BF16)
        mix_wide[...] = jnp.where(same, dot(mix_rows, to_lanes), 0.0).astype(BF16)
        mix_rows = dot_nt(to_rows, mix[...]).astype(BF16)
        mix_wide_t[...] = jnp.where(same, dot(mix_rows, to_lanes), 0.0).astype(BF16)
        bias_wide[...] = dot(bias[...], to_lanes.astype(F32), HIGHEST)
        for part in range(4):
            load(cot_hbm, cot, 4 + part, 4 * part).wait()

    def mix_forward():
        modes = gather_modes(0)
        spectrum[...] = modes
        doubled = dot_nt(modes.astype(BF16), in_wide[...])
        narrow2[...] = doubled
        for beta in range(RANK // 2):
            cols = slice(128 * beta, 128 * beta + 128)
            zed[:, cols] = (joined_wide[:, cols] * doubled).astype(BF16)
        scatter_modes(1, dot(zed[...], out_wide[...]))

    def activate(x, rows_x):
        rhs = jnp.concatenate([mix_wide[...], rows_x], axis=0)
        for y in range(0, NY, 128):
            lhs = jnp.concatenate([field[x, y : y + 128], second[y : y + 128, : 2 * MY]], axis=1)
            combined = dot(lhs, rhs) + bias_wide[...]
            cumulative = 0.5 + 0.5 * lax.erf(combined * math.sqrt(0.5))
            density = jnp.exp2(combined * combined * (-0.5 * math.log2(math.e))) * (1.0 / math.sqrt(2.0 * math.pi))
            act[x, y : y + 128] = (combined * cumulative).astype(BF16)
            derivative = cumulative + combined * density
            up[x, y : y + 128] = (cot[x, y : y + 128].astype(F32) * derivative).astype(BF16)

    def sweep(base, step):
        def body(j, carry):
            for i in range(4):
                x = 4 * j + i
                step(base + x, scratch[pl.ds(x, 2 * MY, stride=HALF), :].astype(BF16))
            return carry

        lax.fori_loop(0, HALF // 4, body, 0)

    def activation():
        total = jnp.zeros((1, FEATS), F32)
        for half in range(2):
            unpack(1, half)
            base = HALF * half

            def after(j, carry, base=base):
                rows = analyse(up, base + 2 * j, 2 * j)
                return carry + rows[0:1, :FEATS] + rows[0:1, FEATS:]

            sweep(base, activate)
            for j in range(HALF // 2):
                total = after(j, total)
            pack(2, half)
            send(2, half)
        rows_sum[...] = total

    def mix_gradient():
        products[...] = jnp.zeros_like(products)

        def accumulate(x, carry):
            products[...] += dot_tn(field[x], up[x])
            return carry

        lax.fori_loop(0, ROWS, accumulate, 0)

    def mix_backward():
        upstream = gather_modes(2)
        upstream_b = upstream.astype(BF16)
        dz = dot_nt(upstream_b, out_wide[...])
        dn = joined_wide[:, 0:128] * dz[:, 0:128]
        for beta in range(1, RANK // 2):
            cols = slice(128 * beta, 128 * beta + 128)
            dn = dn + joined_wide[:, cols] * dz[:, cols]
        return upstream_b, dz, dn.astype(BF16)

    def send_returned(upstream_b, dz, dn_b):
        scatter_modes(3, dot(dn_b, in_wide[...]))

    def fold_tables():
        fold_rank[...] = select((1024, RANK), lambda r, l: l == 2 * (r // 128) + (r % 128) // 64, BF16)
        fold_lanes[...] = select(
            (4 * FEATS, FEATS), lambda r, l: r % C + 32 * (r // FEATS) == l, BF16
        )
        mixed = jnp.where(same, products[...], 0.0) * (MIX_SCALE / CORE_SCALE)
        mixed = (mixed[0:32] + mixed[32:64]) + (mixed[64:96] + mixed[96:128])
        unit = float(np.asarray(1.0 / math.sqrt(NY), dtype=np.float32).astype(jnp.bfloat16))
        biases = rows_sum[...] * (MIX_SCALE / CORE_SCALE / unit)
        fold = select((FEATS, FEATS), lambda r, l: r % C == l)
        fold_bias = select((FEATS, FEATS), lambda r, l: r % C + 64 == l)
        misc[...] = dot(mixed, fold, HIGHEST) + dot(biases, fold_bias, HIGHEST)
        gsend[...] = jnp.zeros_like(gsend)
        hsend[...] = jnp.zeros_like(hsend)

    def core_gradients(upstream_b, dz, dn_b):
        product = jnp.concatenate(
            [dz[:, 128 * b : 128 * b + 128] * narrow2[...] for b in range(RANK // 2)], axis=1
        ).astype(BF16)
        djoined = dot(product, fold_rank[...])
        djoined = (djoined[:MX] + djoined[MX:]).astype(BF16)
        first_part = dot_nt(second_core[...].astype(BF16), djoined)
        second_part = dot(first_core[...].astype(BF16), djoined)
        rows = []
        for beta in range(RANK // 2):
            outer = dot_tn(zed[:, 128 * beta : 128 * beta + 128], upstream_b)
            outer = jnp.where(in_keep, outer, 0.0)
            for base in (0, 64):
                rows.append(
                    (outer[base : base + 16] + outer[base + 16 : base + 32])
                    + (outer[base + 32 : base + 48] + outer[base + 48 : base + 64])
                )
        wide = jnp.concatenate(
            [jnp.concatenate(rows[4 * q : 4 * q + 4], axis=0) for q in range(4)], axis=1
        )
        packed = dot(wide.astype(BF16), fold_lanes[...])
        inner = jnp.where(in_keep, dot_tn(dn_b, spectrum[...].astype(BF16)), 0.0)
        inner = sum(inner[RANK * i : RANK * (i + 1)] for i in range(1, 2 * PLANES)) + inner[0:RANK]
        inner = misc[0:RANK] + dot(inner.astype(BF16), fold_lanes[FEATS : 2 * FEATS])
        for q in range(PARTS):
            gsend[q, 0:2] = packed[2 * q : 2 * q + 2]
        for q in range(RANK):
            gsend[q, 2:3] = inner[q : q + 1]
            gsend[RANK + q, 2:3] = misc[RANK + q : RANK + q + 1]
            gsend[RANK + q, 2:3, 32:64] = first_part[q : q + 1]
        hsend[:, 0:RANK] = second_part

    def to_slice(source, target, sent, received):
        def start(i, carry):
            other = wrap(group + i, GROUPS)
            for y in range(YS):
                to = other * YS + y
                pltpu.make_async_remote_copy(
                    src_ref=source(to), dst_ref=target.at[mine], send_sem=sent, recv_sem=received,
                    device_id={"dp": other, "pencil": y * ZS + z}, device_id_type=MESH,
                ).start()
            return carry

        lax.fori_loop(1, GROUPS, start, 0)
        for i in range(1, YS):
            pencil = wrap(me + i * ZS, PENCILS)
            to = wrap(mine - group * YS + i, YS) + group * YS
            pltpu.make_async_remote_copy(
                src_ref=source(to), dst_ref=target.at[mine], send_sem=sent, recv_sem=received,
                device_id={"pencil": pencil}, device_id_type=MESH,
            ).start()

    def wait_for(target, count, sent, received):
        others = target.at[pl.ds(0, count)]
        return pltpu.make_async_remote_copy(
            src_ref=others, dst_ref=others, send_sem=sent, recv_sem=received,
            device_id={"pencil": lax.rem(me + 1, PENCILS)}, device_id_type=MESH,
        )

    all_slice = wait_for(grecv, PARTS - 1, gssem, grsem)
    all_column = wait_for(brecv, ZS - 1, bssem, brsem)
    all_last = wait_for(grads_out, PARTS - 1, cssem, crsem)
    all_seconds = wait_for(hrecv, GROUPS - 1, hssem, hrsem)

    def sum_slice_send():
        to_slice(lambda to: gsend.at[to], grecv, gssem, grsem)
        grecv[mine] = gsend[mine]

    def sum_slice():
        all_slice.wait_recv()
        chunk = grecv[0]
        for q in range(1, PARTS):
            chunk = chunk + grecv[q]
        bsend[...] = chunk

        def start(i, carry):
            to = column + wrap(z + 1 + i, ZS)
            pltpu.make_async_remote_copy(
                src_ref=bsend, dst_ref=brecv.at[z], send_sem=bssem, recv_sem=brsem,
                device_id={"pencil": to}, device_id_type=MESH,
            ).start()
            return carry

        lax.fori_loop(0, ZS - 1, start, 0)
        brecv[z] = chunk

        def start_second(i, carry):
            pltpu.make_async_remote_copy(
                src_ref=hsend, dst_ref=hrecv.at[group], send_sem=hssem, recv_sem=hrsem,
                device_id={"dp": wrap(group + 1 + i, GROUPS)}, device_id_type=MESH,
            ).start()
            return carry

        lax.fori_loop(0, GROUPS - 1, start_second, 0)
        hrecv[group] = hsend[...]

    def sum_column():
        all_column.wait_recv()
        total = brecv[0]
        for q in range(1, ZS):
            total = total + brecv[q]
        total = total * CORE_SCALE
        csend[...] = total
        to_slice(lambda to: csend, grads_out, cssem, crsem)
        grads_out[mine] = total

    def last():
        all_seconds.wait_recv()
        total = hrecv[0]
        for q in range(1, GROUPS):
            total = total + hrecv[q]
        second_out[...] = total * CORE_SCALE
        all_last.wait_recv()

    def finish(x, rows_x):
        rhs = jnp.concatenate([mix_wide_t[...], rows_x], axis=0)
        for y in range(0, NY, 128):
            lhs = jnp.concatenate([up[x, y : y + 128], second[y : y + 128, : 2 * MY]], axis=1)
            adjoint[x, y : y + 128] = dot(lhs, rhs).astype(BF16)

    def finish_half(half):
        unpack(3, half)
        sweep(HALF * half, finish)

    state = {}
    steps = [
        field_rows, weights, mix_forward, activation, mix_gradient, fold_tables,
        lambda: state.update(modes=mix_backward()),
        lambda: core_gradients(*state["modes"]),
        sum_slice_send, lambda: send_returned(*state["modes"]),
        sum_slice, lambda: finish_half(0), sum_column, lambda: finish_half(1), last,
    ]
    for step in steps[:STOP]:
        step()

    for copy in (all_slice, all_column, all_last, all_seconds):
        copy.wait_send()
    for turn in range(4):
        for half in range(2):
            whole(turn, half).wait_send()


def write_out(
    act, adjoint, grads, second_in,
    act_hbm, adjoint_hbm, first_hbm, second_hbm, output_hbm, input_hbm, mix_hbm, bias_hbm,
    first, second, output, inner, mix, bias, packed, misc, sem,
):
    large = []
    for i in range(4):
        part = pl.ds(ROWS // 4 * i, ROWS // 4)
        large.append(pltpu.make_async_copy(act.at[part], act_hbm.at[part], sem.at[6 + i]))
        large.append(pltpu.make_async_copy(adjoint.at[part], adjoint_hbm.at[part], sem.at[10 + i]))
    for copy in large:
        copy.start()
    second[...] = second_in[:, :RANK]
    for q in range(PARTS):
        packed[2 * q : 2 * q + 2] = grads[q, 0:2]
        misc[q : q + 1] = grads[q, 2:3]
    for quarter in range(4):
        output[64 * quarter : 64 * quarter + 64] = packed[:, 32 * quarter : 32 * quarter + 32]
    mix[...] = misc[:, 0:32]
    inner[...] = misc[0:RANK, 32:64]
    first[...] = misc[RANK:C, 32:64]
    bias[...] = misc[0:1, 64:96]
    pairs = [
        (first, first_hbm), (second, second_hbm), (output, output_hbm),
        (inner, input_hbm), (mix, mix_hbm), (bias, bias_hbm),
    ]
    small = [pltpu.make_async_copy(a, b, sem.at[i]) for i, (a, b) in enumerate(pairs)]
    for copy in small:
        copy.start()
    for copy in large + small:
        copy.wait()


def shards(field, cotangent, first_core, second_core, output_core, input_core, channel_mix, channel_bias):
    slab = (ROWS, NY, FEATS)
    vmem = pl.BlockSpec(memory_space=pltpu.VMEM)
    hbm = pl.BlockSpec(memory_space=pltpu.HBM)
    dma = pltpu.SemaphoreType.DMA
    smalls = [(RANK, MX), (RANK, RANK), (RANK * RANK, C), (RANK, C), (C, C), (1, C)]
    types = [F32, F32, F32, F32, BF16, F32]
    act, adjoint, grads, second_total = pl.pallas_call(
        kernel,
        out_shape=[
            jax.ShapeDtypeStruct(slab, BF16),
            jax.ShapeDtypeStruct(slab, BF16),
            jax.ShapeDtypeStruct((PARTS, CHUNK, FEATS), F32),
            jax.ShapeDtypeStruct((16, FEATS), F32),
        ],
        in_specs=[hbm] * 9,
        out_specs=[vmem] * 4,
        scratch_shapes=[
            pltpu.VMEM(slab, BF16),
            pltpu.VMEM(slab, BF16),
            pltpu.VMEM(slab, BF16),
            pltpu.VMEM((BLOCK, FEATS), F32),
            pltpu.VMEM((BLOCK, FEATS), F32),
            pltpu.VMEM((4, 2, PENCILS, MESSAGE, FEATS), BF16),
            pltpu.VMEM((4, 2, PENCILS, MESSAGE, FEATS), BF16),
        ]
        + [pltpu.VMEM(s, t) for s, t in zip(smalls, types)]
        + [
            pltpu.VMEM((2 * MY, NY), BF16),
            pltpu.VMEM((2 * MX, 2 * NX), BF16),
            pltpu.VMEM((NY, FEATS), BF16),
            pltpu.VMEM((2 * NX, FEATS), BF16),
            pltpu.VMEM((2 * MX, 1024), F32),
            pltpu.VMEM((1024, FEATS), BF16),
            pltpu.VMEM((FEATS, FEATS), BF16),
            pltpu.VMEM((FEATS, FEATS), BF16),
            pltpu.VMEM((FEATS, FEATS), BF16),
            pltpu.VMEM((1, FEATS), F32),
            pltpu.VMEM((2 * MX, FEATS), F32),
            pltpu.VMEM((2 * MX, 1024), BF16),
            pltpu.VMEM((2 * MX, FEATS), F32),
            pltpu.VMEM((FEATS, FEATS), F32),
            pltpu.VMEM((1, FEATS), F32),
            pltpu.VMEM((1024, RANK), BF16),
            pltpu.VMEM((4 * FEATS, FEATS), BF16),
            pltpu.VMEM((C, FEATS), F32),
            pltpu.VMEM((PARTS, CHUNK, FEATS), F32),
            pltpu.VMEM((PARTS, CHUNK, FEATS), F32),
            pltpu.VMEM((CHUNK, FEATS), F32),
            pltpu.VMEM((ZS, CHUNK, FEATS), F32),
            pltpu.VMEM((CHUNK, FEATS), F32),
            pltpu.VMEM((RANK, FEATS), F32),
            pltpu.VMEM((GROUPS, RANK, FEATS), F32),
            dma((8,)),
            dma((20,)),
            dma((4, 2)),
            dma((4, 2)),
            dma,
            dma,
            dma,
            dma,
            dma,
            dma,
            dma,
            dma,
        ],
        compiler_params=pltpu.CompilerParams(
            collective_id=0, has_side_effects=True, vmem_limit_bytes=40 * 2**20
        ),
    )(
        *[
            pltpu.with_memory_space_constraint(a, pltpu.HBM)
            for a in (
                field[0],
                cotangent[0],
                first_core.T,
                second_core[:, 0, :],
                output_core.transpose(0, 2, 1).reshape(RANK * RANK, C),
                input_core,
                channel_mix,
                channel_bias[None],
                jnp.asarray(tables()),
            )
        ]
    )
    results = pl.pallas_call(
        write_out,
        out_shape=[jax.ShapeDtypeStruct(slab, BF16), jax.ShapeDtypeStruct(slab, BF16)]
        + [jax.ShapeDtypeStruct(s, F32) for s in smalls],
        in_specs=[vmem] * 4,
        out_specs=[hbm] * 8,
        scratch_shapes=[pltpu.VMEM(s, F32) for s in smalls + [(64, FEATS), (C, FEATS)]] + [dma((14,))],
        compiler_params=pltpu.CompilerParams(vmem_limit_bytes=16 * 2**20),
    )(act, adjoint, grads, second_total)
    act, adjoint, first, second, output, inner, mix, bias = results
    return (
        act[None],
        adjoint[None],
        first.T,
        second[:, None, :],
        output.reshape(RANK, RANK, C).transpose(0, 2, 1),
        inner,
        mix,
        bias[0],
    )


def solution(mesh):
    slabs = P("dp", "pencil", None, None)
    column = P(None, "pencil", None)
    return jax.shard_map(
        shards,
        mesh=mesh,
        in_specs=(slabs, slabs, P(), column, P(), P(), P(), P()),
        out_specs=(slabs, slabs, P(), column, P(), P(), P(), P()),
        check_vma=False,
    )
```

```python
import math

import jax
import jax.numpy as jnp
import numpy as np
from jax import lax
from jax.experimental import pallas as pl
from jax.experimental.pallas import tpu as pltpu
from jax.sharding import PartitionSpec as P

F32 = jnp.float32
BF16 = jnp.bfloat16
MESH = pl.DeviceIdType.MESH
HIGHEST = lax.Precision.HIGHEST

NX = 512
NY = 512
C = 32
MX = 32
MY = 32
RANK = 16
PLANES = 4
GROUPS = 8
FEATS = 128
PENCILS = 32
ROWS = NX // PENCILS
HALF = ROWS // 2
MESSAGE = 2 * HALF
BLOCK = PENCILS * MESSAGE
CHUNK = 16
FARTHEST = sorted(
    [(y, z) for y in range(4) for z in range(8) if y + z],
    key=lambda step: (-min(step[0], 4 - step[0]) - min(step[1], 8 - step[1]), step),
)
CORE_SCALE = 1.0 / math.sqrt(GROUPS * PLANES * MX * MY)
MIX_SCALE = 1.0 / math.sqrt(GROUPS * PLANES * NX * NY)


def tables():
    y = np.arange(NY, dtype=np.int64)
    m = np.arange(MY, dtype=np.int64)
    angles = (y[:, None] * m[None, :] % NY) * (2.0 * math.pi / NY)
    factor = 1.0 / math.sqrt(NY)
    second = np.stack([np.cos(angles) * factor, -np.sin(angles) * factor], axis=2).reshape(NY, 2 * MY)
    x = np.arange(NX, dtype=np.int64)
    k = np.arange(MX, dtype=np.int64)
    angles = (k[:, None] * x[None, :] % NX) * (2.0 * math.pi / NX)
    factor = 1.0 / math.sqrt(NX)
    a, b = np.cos(angles) * factor, np.sin(angles) * factor
    first = np.concatenate([np.concatenate([a, b], axis=1), np.concatenate([-b, a], axis=1)], axis=0)
    first = first.reshape(2 * MX, 2, PENCILS, 2, HALF).transpose(0, 3, 2, 1, 4).reshape(2 * MX, 2 * NX)
    pad = np.zeros((NY, FEATS - 2 * MY))
    pieces = (
        [second[FEATS * i : FEATS * (i + 1)].T for i in range(NY // FEATS)]
        + [first[:, FEATS * i : FEATS * (i + 1)] for i in range(2 * NX // FEATS)]
        + [np.concatenate([second, pad], axis=1)]
        + [np.concatenate([first.T, np.concatenate([pad, pad])], axis=1)]
    )
    return np.concatenate(pieces, axis=0).astype(np.float32).astype(jnp.bfloat16)


def dot(a, b, precision=None):
    return jnp.dot(a, b, preferred_element_type=F32, precision=precision)


def dot_nt(a, b):
    return lax.dot_general(a, b, (((1,), (1,)), ((), ())), preferred_element_type=F32)


def dot_tn(a, b, precision=None):
    return lax.dot_general(a, b, (((0,), (0,)), ((), ())), preferred_element_type=F32, precision=precision)


def iotas(shape):
    return lax.broadcasted_iota(jnp.int32, shape, 0), lax.broadcasted_iota(jnp.int32, shape, 1)


def select(shape, rule, dtype=F32):
    rows, lanes = iotas(shape)
    return jnp.where(rule(rows, lanes), 1.0, 0.0).astype(dtype)


def kernel(
    field_hbm, cot_hbm, first_hbm, second_hbm, output_hbm, input_hbm, mix_hbm, bias_hbm, table_hbm,
    act, adjoint, grads_out, second_out,
    field, cot, up, scratch, analysed, sbuf, rbuf,
    first_core, second_core, output_core, input_core, mix, bias, second_t, first, second, first_t,
    joined_wide, out_wide, in_wide, mix_wide, mix_wide_t, bias_wide, narrow2, zed, spectrum, products, rows_sum, fold_rank, fold_lanes, misc,
    rest, gsend, grecv, bsend, brecv, csend,
    load_sem, small_sem, ssem, rsem, gssem, grsem, bssem, brsem, cssem, crsem,
):
    me = lax.axis_index("pencil")
    group = lax.axis_index("dp")
    spot = lax.rem(me, 8)
    row = me - spot

    def load(source, target, slot, x):
        return pltpu.make_async_copy(source.at[pl.ds(x, 4)], target.at[pl.ds(x, 4)], load_sem.at[slot])

    smalls = []
    for i in range(NY // FEATS):
        smalls.append((table_hbm.at[pl.ds(64 * i, 64)], second_t.at[:, pl.ds(FEATS * i, FEATS)]))
    for i in range(2 * NX // FEATS):
        smalls.append((table_hbm.at[pl.ds(256 + 64 * i, 64)], first.at[:, pl.ds(FEATS * i, FEATS)]))
    smalls.append((table_hbm.at[pl.ds(768, NY)], second))
    smalls.append((table_hbm.at[pl.ds(768 + NY, 2 * NX)], first_t))
    smalls += [
        (first_hbm, first_core), (second_hbm, second_core), (output_hbm, output_core),
        (input_hbm, input_core), (mix_hbm, mix), (bias_hbm, bias),
    ]
    copies = [pltpu.make_async_copy(a, b, small_sem.at[i]) for i, (a, b) in enumerate(smalls)]

    for copy in copies[:4]:
        copy.start()
    load(field_hbm, field, 0, 0).start()
    barrier = pltpu.get_barrier_semaphore()

    def wrap(i, size):
        return jnp.where(i >= size, i - size, i)

    greeted = [{"pencil": wrap(me + i, PENCILS)} for i in range(1, PENCILS)]
    greeted += [{"dp": wrap(group + i, GROUPS)} for i in range(1, GROUPS)]
    for to in greeted:
        pl.semaphore_signal(barrier, inc=1, device_id=to, device_id_type=MESH)
    for part in range(1, 4):
        load(field_hbm, field, part, 4 * part).start()
    for copy in copies[4:]:
        copy.start()
    for part in range(4):
        load(cot_hbm, cot, 4 + part, 4 * part).start()

    def send(turn, half):
        for dy, dz in FARTHEST:
            to = wrap(row + dy * 8, PENCILS) + wrap(spot + dz, 8)
            pltpu.make_async_remote_copy(
                src_ref=sbuf.at[turn, half, to],
                dst_ref=rbuf.at[turn, half, me],
                send_sem=ssem.at[turn, half],
                recv_sem=rsem.at[turn, half],
                device_id={"pencil": to},
                device_id_type=MESH,
            ).start()
        rbuf[turn, half, me] = sbuf[turn, half, me]

    def whole(turn, half):
        return pltpu.make_async_remote_copy(
            src_ref=sbuf.at[turn, half, pl.ds(0, PENCILS - 1)],
            dst_ref=rbuf.at[turn, half, pl.ds(0, PENCILS - 1)],
            send_sem=ssem.at[turn, half],
            recv_sem=rsem.at[turn, half],
            device_id={"pencil": lax.rem(me + 1, PENCILS)},
            device_id_type=MESH,
        )

    def analyse(source, x, x_half):
        pair = jnp.concatenate([source[x], source[x + 1]], axis=1)
        rows = dot(second_t[...], pair)
        analysed[pl.ds(x_half, 2 * MY, stride=HALF), :] = rows[:, :FEATS]
        analysed[pl.ds(x_half + 1, 2 * MY, stride=HALF), :] = rows[:, FEATS:]
        return rows

    def pack(turn, half):
        sbuf[turn, half] = analysed[...].astype(BF16).reshape(PENCILS, MESSAGE, FEATS)

    def gather_modes(turn):
        total = None
        for half in range(2):
            whole(turn, half).wait_recv()
            term = dot(first[:, BLOCK * half : BLOCK * (half + 1)], rbuf[turn, half].reshape(BLOCK, FEATS))
            total = term if total is None else total + term
        return total

    def scatter_modes(turn, modes):
        narrow = modes.astype(BF16)
        for half in range(2):
            rows = dot(first_t[BLOCK * half : BLOCK * (half + 1), : 2 * MX], narrow)
            sbuf[turn, half] = rows.astype(BF16).reshape(PENCILS, MESSAGE, FEATS)
            send(turn, half)

    def unpack(turn, half):
        whole(turn, half).wait_recv()
        scratch[...] = rbuf[turn, half].astype(F32).reshape(BLOCK, FEATS)

    rows128, lanes128 = iotas((FEATS, FEATS))
    same = rows128 // C == lanes128 // C
    in_keep = (rows128 % 64) // RANK == lanes128 // C

    def field_rows():
        for copy in copies[:4]:
            copy.wait()
        for half in range(2):
            for part in range(2):
                load(field_hbm, field, 2 * half + part, HALF * half + 4 * part).wait()
                for x in range(4 * part, 4 * part + 4, 2):
                    analyse(field, HALF * half + x, x)
            pack(0, half)
        pl.semaphore_wait(barrier, len(greeted))
        for half in range(2):
            send(0, half)

    def weights():
        for copy in copies[4:]:
            copy.wait()
        joined = dot_tn(first_core[...], second_core[...], HIGHEST)
        joined2 = jnp.concatenate([joined, joined], axis=0)
        spread = select((RANK, 1024), lambda r, l: r == 2 * (l // 128) + (l % 128) // 64)
        joined_wide[...] = dot(joined2, spread, HIGHEST)
        to_lanes = select((C, FEATS), lambda r, l: r == l % C, BF16)
        to_rows = select((FEATS, C), lambda r, l: r % C == l, BF16)
        pair_rows = select((FEATS, RANK), lambda r, l: r % RANK == l, BF16)
        for beta in range(RANK // 2):
            rows = output_core[2 * RANK * beta : 2 * RANK * beta + 2 * RANK].astype(BF16)
            low, high = rows[:RANK], rows[RANK:]
            tall = jnp.concatenate([low] * PLANES + [high] * PLANES, axis=0)
            wide = jnp.where(in_keep, dot(tall, to_lanes), 0.0)
            out_wide[128 * beta : 128 * beta + 128, :] = wide.astype(BF16)
        in_rows = dot(pair_rows, input_core[...].astype(BF16)).astype(BF16)
        in_wide[...] = jnp.where(in_keep, dot(in_rows, to_lanes), 0.0).astype(BF16)
        mix_rows = dot(to_rows, mix[...]).astype(BF16)
        mix_wide[...] = jnp.where(same, dot(mix_rows, to_lanes), 0.0).astype(BF16)
        mix_rows = dot_nt(to_rows, mix[...]).astype(BF16)
        mix_wide_t[...] = jnp.where(same, dot(mix_rows, to_lanes), 0.0).astype(BF16)
        bias_wide[...] = dot(bias[...], to_lanes.astype(F32), HIGHEST)
        for part in range(4):
            load(cot_hbm, cot, 4 + part, 4 * part).wait()

    def mix_forward():
        modes = gather_modes(0)
        spectrum[...] = modes
        doubled = dot_nt(modes.astype(BF16), in_wide[...])
        narrow2[...] = doubled
        for beta in range(RANK // 2):
            cols = slice(128 * beta, 128 * beta + 128)
            zed[:, cols] = (joined_wide[:, cols] * doubled).astype(BF16)
        scatter_modes(1, dot(zed[...], out_wide[...]))

    def activate(x, rows_x):
        rhs = jnp.concatenate([mix_wide[...], rows_x], axis=0)
        for y in range(0, NY, 128):
            lhs = jnp.concatenate([field[x, y : y + 128], second[y : y + 128, : 2 * MY]], axis=1)
            combined = dot(lhs, rhs) + bias_wide[...]
            cumulative = 0.5 + 0.5 * lax.erf(combined * math.sqrt(0.5))
            density = jnp.exp2(combined * combined * (-0.5 * math.log2(math.e))) * (1.0 / math.sqrt(2.0 * math.pi))
            act[x, y : y + 128] = (combined * cumulative).astype(BF16)
            derivative = cumulative + combined * density
            up[x, y : y + 128] = (cot[x, y : y + 128].astype(F32) * derivative).astype(BF16)

    def sweep(base, step):
        def body(j, carry):
            for i in range(4):
                x = 4 * j + i
                step(base + x, scratch[pl.ds(x, 2 * MY, stride=HALF), :].astype(BF16))
            return carry

        lax.fori_loop(0, HALF // 4, body, 0)

    def activation():
        total = jnp.zeros((1, FEATS), F32)
        for half in range(2):
            unpack(1, half)
            base = HALF * half

            def after(j, carry, base=base):
                rows = analyse(up, base + 2 * j, 2 * j)
                return carry + rows[0:1, :FEATS] + rows[0:1, FEATS:]

            sweep(base, activate)
            for j in range(HALF // 2):
                total = after(j, total)
            pack(2, half)
            send(2, half)
        rows_sum[...] = total

    def mix_gradient():
        products[...] = jnp.zeros_like(products)

        def accumulate(x, carry):
            products[...] += dot_tn(field[x], up[x])
            return carry

        lax.fori_loop(0, ROWS, accumulate, 0)

    def mix_backward():
        upstream = gather_modes(2)
        upstream_b = upstream.astype(BF16)
        dz = dot_nt(upstream_b, out_wide[...])
        dn = joined_wide[:, 0:128] * dz[:, 0:128]
        for beta in range(1, RANK // 2):
            cols = slice(128 * beta, 128 * beta + 128)
            dn = dn + joined_wide[:, cols] * dz[:, cols]
        return upstream_b, dz, dn.astype(BF16)

    def send_returned(upstream_b, dz, dn_b):
        scatter_modes(3, dot(dn_b, in_wide[...]))

    def fold_tables():
        fold_rank[...] = select(
            (1024, FEATS), lambda r, l: l % RANK == 2 * (r // 128) + (r % 128) // 64, BF16
        )
        fold_lanes[...] = select(
            (4 * FEATS, FEATS), lambda r, l: r % C + 32 * (r // FEATS) == l, BF16
        )
        mixed = jnp.where(same, products[...], 0.0) * (MIX_SCALE / CORE_SCALE)
        mixed = (mixed[0:32] + mixed[32:64]) + (mixed[64:96] + mixed[96:128])
        unit = float(np.asarray(1.0 / math.sqrt(NY), dtype=np.float32).astype(jnp.bfloat16))
        biases = rows_sum[...] * (MIX_SCALE / CORE_SCALE / unit)
        fold = select((FEATS, FEATS), lambda r, l: r % C == l)
        fold_bias = select((FEATS, FEATS), lambda r, l: r % C + 64 == l)
        misc[...] = dot(mixed, fold, HIGHEST) + dot(biases, fold_bias, HIGHEST)

    def core_gradients(upstream_b, dz, dn_b):
        product = jnp.concatenate(
            [dz[:, 128 * b : 128 * b + 128] * narrow2[...] for b in range(RANK // 2)], axis=1
        ).astype(BF16)
        djoined = dot(product, fold_rank[...])
        djoined = (djoined[:MX] + djoined[MX:]).astype(BF16)
        first_part = dot_nt(second_core[...].astype(BF16), djoined[:, :RANK])
        second_part = dot(first_core[...].astype(BF16), djoined)
        rows16, lanes16 = iotas((RANK, FEATS))
        second_part = jnp.where(rows16 % 8 == lanes16 // RANK, second_part, 0.0)
        second_part = jnp.concatenate(
            [jnp.sum(second_part[8 * i : 8 * i + 8], axis=0, keepdims=True) for i in range(2)], axis=0
        )
        rows = []
        for beta in range(RANK // 2):
            outer = dot_tn(zed[:, 128 * beta : 128 * beta + 128], upstream_b)
            outer = jnp.where(in_keep, outer, 0.0)
            for base in (0, 64):
                rows.append(
                    (outer[base : base + 16] + outer[base + 16 : base + 32])
                    + (outer[base + 32 : base + 48] + outer[base + 48 : base + 64])
                )
        wide = jnp.concatenate(
            [jnp.concatenate(rows[4 * q : 4 * q + 4], axis=0) for q in range(4)], axis=1
        )
        packed = dot(wide.astype(BF16), fold_lanes[...])
        inner = jnp.where(in_keep, dot_tn(dn_b, spectrum[...].astype(BF16)), 0.0)
        inner = sum(inner[RANK * i : RANK * (i + 1)] for i in range(1, 2 * PLANES)) + inner[0:RANK]
        inner = misc[0:RANK] + dot(inner.astype(BF16), fold_lanes[FEATS : 2 * FEATS])
        rest[...] = misc[...]
        rest[0:RANK] = inner
        rest[RANK:C, 32:64] = first_part
        for q in range(GROUPS):
            parts = [packed[8 * q : 8 * q + 8], rest[4 * q : 4 * q + 4], second_part, jnp.zeros((2, FEATS), F32)]
            gsend[q] = jnp.concatenate(parts, axis=0).astype(BF16)

    def to_groups(source, target, sent, received):
        def start(i, carry):
            to = wrap(group + i, GROUPS)
            pltpu.make_async_remote_copy(
                src_ref=source(to), dst_ref=target.at[group], send_sem=sent, recv_sem=received,
                device_id={"dp": to}, device_id_type=MESH,
            ).start()
            return carry

        lax.fori_loop(1, GROUPS, start, 0, unroll=True)

    def wait_for(target, count, sent, received):
        others = target.at[pl.ds(0, count)]
        return pltpu.make_async_remote_copy(
            src_ref=others, dst_ref=others, send_sem=sent, recv_sem=received,
            device_id={"pencil": lax.rem(me + 1, PENCILS)}, device_id_type=MESH,
        )

    all_groups = wait_for(grecv, GROUPS - 1, gssem, grsem)
    all_pencils = wait_for(brecv, PENCILS - 1, bssem, brsem)
    all_last = wait_for(grads_out, GROUPS - 1, cssem, crsem)

    def sum_groups_send():
        to_groups(lambda to: gsend.at[to], grecv, gssem, grsem)
        grecv[group] = gsend[group]

    def sum_groups():
        all_groups.wait_recv()
        chunk = grecv[0].astype(F32)
        for q in range(1, GROUPS):
            chunk = chunk + grecv[q].astype(F32)
        second_out[...] = chunk * CORE_SCALE
        bsend[...] = chunk.astype(BF16)

        def start(i, carry):
            pltpu.make_async_remote_copy(
                src_ref=bsend, dst_ref=brecv.at[me], send_sem=bssem, recv_sem=brsem,
                device_id={"pencil": wrap(me + 1 + i, PENCILS)}, device_id_type=MESH,
            ).start()
            return carry

        lax.fori_loop(0, PENCILS - 1, start, 0, unroll=4)
        brecv[me] = bsend[...]

    def sum_pencils():
        all_pencils.wait_recv()
        total = brecv[0].astype(F32)
        for q in range(1, PENCILS):
            total = total + brecv[q].astype(F32)
        total = total * CORE_SCALE
        csend[...] = total
        to_groups(lambda to: csend, grads_out, cssem, crsem)
        grads_out[group] = total

    def last():
        all_last.wait_recv()

    def finish(x, rows_x):
        rhs = jnp.concatenate([mix_wide_t[...], rows_x], axis=0)
        for y in range(0, NY, 128):
            lhs = jnp.concatenate([up[x, y : y + 128], second[y : y + 128, : 2 * MY]], axis=1)
            adjoint[x, y : y + 128] = dot(lhs, rhs).astype(BF16)

    def finish_half(half):
        unpack(3, half)
        sweep(HALF * half, finish)

    state = {}
    steps = [
        field_rows, weights, mix_forward, activation, mix_gradient, fold_tables,
        lambda: state.update(modes=mix_backward()),
        lambda: core_gradients(*state["modes"]),
        sum_groups_send, lambda: send_returned(*state["modes"]),
        sum_groups, lambda: finish_half(0), sum_pencils, lambda: finish_half(1), last,
    ]
    for step in steps:
        step()

    for copy in (all_groups, all_pencils, all_last):
        copy.wait_send()
    for turn in range(4):
        for half in range(2):
            whole(turn, half).wait_send()


def write_out(
    act, adjoint, grads, second_in,
    act_hbm, adjoint_hbm, first_hbm, second_hbm, output_hbm, input_hbm, mix_hbm, bias_hbm,
    first, second, output, inner, mix, bias, packed, misc, sem,
):
    large = []
    for i in range(4):
        part = pl.ds(ROWS // 4 * i, ROWS // 4)
        large.append(pltpu.make_async_copy(act.at[part], act_hbm.at[part], sem.at[6 + i]))
        large.append(pltpu.make_async_copy(adjoint.at[part], adjoint_hbm.at[part], sem.at[10 + i]))
    for copy in large:
        copy.start()
    for i in range(RANK):
        second[i : i + 1] = second_in[12 + i // 8 : 13 + i // 8, RANK * (i % 8) : RANK * (i % 8) + RANK]
    for q in range(GROUPS):
        packed[8 * q : 8 * q + 8] = grads[q, 0:8]
        misc[4 * q : 4 * q + 4] = grads[q, 8:12]
    for quarter in range(4):
        output[64 * quarter : 64 * quarter + 64] = packed[:, 32 * quarter : 32 * quarter + 32]
    mix[...] = misc[:, 0:32]
    inner[...] = misc[0:RANK, 32:64]
    first[...] = misc[RANK:C, 32:64]
    bias[...] = misc[0:1, 64:96]
    pairs = [
        (first, first_hbm), (second, second_hbm), (output, output_hbm),
        (inner, input_hbm), (mix, mix_hbm), (bias, bias_hbm),
    ]
    small = [pltpu.make_async_copy(a, b, sem.at[i]) for i, (a, b) in enumerate(pairs)]
    for copy in small:
        copy.start()
    for copy in large + small:
        copy.wait()


def shards(field, cotangent, first_core, second_core, output_core, input_core, channel_mix, channel_bias):
    slab = (ROWS, NY, FEATS)
    vmem = pl.BlockSpec(memory_space=pltpu.VMEM)
    hbm = pl.BlockSpec(memory_space=pltpu.HBM)
    dma = pltpu.SemaphoreType.DMA
    smalls = [(RANK, MX), (RANK, RANK), (RANK * RANK, C), (RANK, C), (C, C), (1, C)]
    types = [F32, F32, F32, F32, BF16, F32]
    act, adjoint, grads, second_total = pl.pallas_call(
        kernel,
        out_shape=[
            jax.ShapeDtypeStruct(slab, BF16),
            jax.ShapeDtypeStruct(slab, BF16),
            jax.ShapeDtypeStruct((GROUPS, CHUNK, FEATS), F32),
            jax.ShapeDtypeStruct((16, FEATS), F32),
        ],
        in_specs=[hbm] * 9,
        out_specs=[vmem] * 4,
        scratch_shapes=[
            pltpu.VMEM(slab, BF16),
            pltpu.VMEM(slab, BF16),
            pltpu.VMEM(slab, BF16),
            pltpu.VMEM((BLOCK, FEATS), F32),
            pltpu.VMEM((BLOCK, FEATS), F32),
            pltpu.VMEM((4, 2, PENCILS, MESSAGE, FEATS), BF16),
            pltpu.VMEM((4, 2, PENCILS, MESSAGE, FEATS), BF16),
        ]
        + [pltpu.VMEM(s, t) for s, t in zip(smalls, types)]
        + [
            pltpu.VMEM((2 * MY, NY), BF16),
            pltpu.VMEM((2 * MX, 2 * NX), BF16),
            pltpu.VMEM((NY, FEATS), BF16),
            pltpu.VMEM((2 * NX, FEATS), BF16),
            pltpu.VMEM((2 * MX, 1024), F32),
            pltpu.VMEM((1024, FEATS), BF16),
            pltpu.VMEM((FEATS, FEATS), BF16),
            pltpu.VMEM((FEATS, FEATS), BF16),
            pltpu.VMEM((FEATS, FEATS), BF16),
            pltpu.VMEM((1, FEATS), F32),
            pltpu.VMEM((2 * MX, FEATS), F32),
            pltpu.VMEM((2 * MX, 1024), BF16),
            pltpu.VMEM((2 * MX, FEATS), F32),
            pltpu.VMEM((FEATS, FEATS), F32),
            pltpu.VMEM((1, FEATS), F32),
            pltpu.VMEM((1024, FEATS), BF16),
            pltpu.VMEM((4 * FEATS, FEATS), BF16),
            pltpu.VMEM((C, FEATS), F32),
            pltpu.VMEM((C, FEATS), F32),
            pltpu.VMEM((GROUPS, CHUNK, FEATS), BF16),
            pltpu.VMEM((GROUPS, CHUNK, FEATS), BF16),
            pltpu.VMEM((CHUNK, FEATS), BF16),
            pltpu.VMEM((PENCILS, CHUNK, FEATS), BF16),
            pltpu.VMEM((CHUNK, FEATS), F32),
            dma((8,)),
            dma((20,)),
            dma((4, 2)),
            dma((4, 2)),
            dma,
            dma,
            dma,
            dma,
            dma,
            dma,
        ],
        compiler_params=pltpu.CompilerParams(
            collective_id=0, has_side_effects=True, vmem_limit_bytes=40 * 2**20
        ),
    )(
        *[
            pltpu.with_memory_space_constraint(a, pltpu.HBM)
            for a in (
                field[0],
                cotangent[0],
                first_core.T,
                second_core[:, 0, :],
                output_core.transpose(0, 2, 1).reshape(RANK * RANK, C),
                input_core,
                channel_mix,
                channel_bias[None],
                jnp.asarray(tables()),
            )
        ]
    )
    results = pl.pallas_call(
        write_out,
        out_shape=[jax.ShapeDtypeStruct(slab, BF16), jax.ShapeDtypeStruct(slab, BF16)]
        + [jax.ShapeDtypeStruct(s, F32) for s in smalls],
        in_specs=[vmem] * 4,
        out_specs=[hbm] * 8,
        scratch_shapes=[pltpu.VMEM(s, F32) for s in smalls + [(64, FEATS), (C, FEATS)]] + [dma((14,))],
        compiler_params=pltpu.CompilerParams(vmem_limit_bytes=16 * 2**20),
    )(act, adjoint, grads, second_total)
    act, adjoint, first, second, output, inner, mix, bias = results
    return (
        act[None],
        adjoint[None],
        first.T,
        second[:, None, :],
        output.reshape(RANK, RANK, C).transpose(0, 2, 1),
        inner,
        mix,
        bias[0],
    )


def solution(mesh):
    slabs = P("dp", "pencil", None, None)
    column = P(None, "pencil", None)
    return jax.shard_map(
        shards,
        mesh=mesh,
        in_specs=(slabs, slabs, P(), column, P(), P(), P(), P()),
        out_specs=(slabs, slabs, P(), column, P(), P(), P(), P()),
        check_vma=False,
    )
```

```python
import math

import jax
import jax.numpy as jnp
import numpy as np
from jax import lax
from jax.experimental import pallas as pl
from jax.experimental.pallas import tpu as pltpu
from jax.sharding import PartitionSpec as P

F32 = jnp.float32
BF16 = jnp.bfloat16
MESH = pl.DeviceIdType.MESH
HIGHEST = lax.Precision.HIGHEST

NX = 512
NY = 512
C = 32
MX = 32
MY = 32
RANK = 16
PLANES = 4
GROUPS = 8
FEATS = 128
PENCILS = 32
ROWS = NX // PENCILS
HALF = ROWS // 2
MESSAGE = 2 * HALF
BLOCK = PENCILS * MESSAGE
CHUNK = 16
FARTHEST = sorted(
    [(y, z) for y in range(4) for z in range(8) if y + z],
    key=lambda step: (-2 * min(step[0], 4 - step[0]) - min(step[1], 8 - step[1]), step),
)
CORE_SCALE = 1.0 / math.sqrt(GROUPS * PLANES * MX * MY)
MIX_SCALE = 1.0 / math.sqrt(GROUPS * PLANES * NX * NY)


def tables():
    y = np.arange(NY, dtype=np.int64)
    m = np.arange(MY, dtype=np.int64)
    angles = (y[:, None] * m[None, :] % NY) * (2.0 * math.pi / NY)
    factor = 1.0 / math.sqrt(NY)
    second = np.stack([np.cos(angles) * factor, -np.sin(angles) * factor], axis=2).reshape(NY, 2 * MY)
    x = np.arange(NX, dtype=np.int64)
    k = np.arange(MX, dtype=np.int64)
    angles = (k[:, None] * x[None, :] % NX) * (2.0 * math.pi / NX)
    factor = 1.0 / math.sqrt(NX)
    a, b = np.cos(angles) * factor, np.sin(angles) * factor
    first = np.concatenate([np.concatenate([a, b], axis=1), np.concatenate([-b, a], axis=1)], axis=0)
    first = first.reshape(2 * MX, 2, PENCILS, 2, HALF).transpose(0, 3, 2, 1, 4).reshape(2 * MX, 2 * NX)
    pad = np.zeros((NY, FEATS - 2 * MY))
    ones = pad + (np.arange(FEATS - 2 * MY) < 3)
    pieces = (
        [second[FEATS * i : FEATS * (i + 1)].T for i in range(NY // FEATS)]
        + [first[:, FEATS * i : FEATS * (i + 1)] for i in range(2 * NX // FEATS)]
        + [np.concatenate([second, ones], axis=1)]
        + [np.concatenate([first.T, np.concatenate([pad, pad])], axis=1)]
    )
    return np.concatenate(pieces, axis=0).astype(np.float32).astype(jnp.bfloat16)


def dot(a, b, precision=None):
    return jnp.dot(a, b, preferred_element_type=F32, precision=precision)


def dot_nt(a, b):
    return lax.dot_general(a, b, (((1,), (1,)), ((), ())), preferred_element_type=F32)


def dot_tn(a, b, precision=None):
    return lax.dot_general(a, b, (((0,), (0,)), ((), ())), preferred_element_type=F32, precision=precision)


def iotas(shape):
    return lax.broadcasted_iota(jnp.int32, shape, 0), lax.broadcasted_iota(jnp.int32, shape, 1)


def select(shape, rule, dtype=F32):
    rows, lanes = iotas(shape)
    return jnp.where(rule(rows, lanes), 1.0, 0.0).astype(dtype)


def kernel(
    field_hbm, cot_hbm, first_hbm, second_hbm, output_hbm, input_hbm, mix_hbm, bias_hbm, table_hbm,
    act, adjoint, grads_out, second_out,
    field, cot, up, scratch, analysed, sbuf, rbuf,
    first_core, second_core, output_core, input_core, mix, bias, second_t, first, second, first_t,
    joined_wide, out_wide, in_wide, mix_wide, mix_wide_t, bias_rows, narrow2, zed, spectrum, products, rows_sum, fold_rank, fold_lanes, misc,
    rest, gsend, grecv, bsend, brecv, csend,
    load_sem, small_sem, ssem, rsem, gssem, grsem, bssem, brsem, cssem, crsem,
):
    me = lax.axis_index("pencil")
    group = lax.axis_index("dp")
    spot = lax.rem(me, 8)
    row = me - spot

    def load(source, target, slot, x):
        return pltpu.make_async_copy(source.at[pl.ds(x, 4)], target.at[pl.ds(x, 4)], load_sem.at[slot])

    smalls = []
    for i in range(NY // FEATS):
        smalls.append((table_hbm.at[pl.ds(64 * i, 64)], second_t.at[:, pl.ds(FEATS * i, FEATS)]))
    for i in range(2 * NX // FEATS):
        smalls.append((table_hbm.at[pl.ds(256 + 64 * i, 64)], first.at[:, pl.ds(FEATS * i, FEATS)]))
    smalls.append((table_hbm.at[pl.ds(768, NY)], second))
    smalls.append((table_hbm.at[pl.ds(768 + NY, 2 * NX)], first_t))
    smalls += [
        (first_hbm, first_core), (second_hbm, second_core), (output_hbm, output_core),
        (input_hbm, input_core), (mix_hbm, mix), (bias_hbm, bias),
    ]
    copies = [pltpu.make_async_copy(a, b, small_sem.at[i]) for i, (a, b) in enumerate(smalls)]

    for copy in copies[:4]:
        copy.start()
    load(field_hbm, field, 0, 0).start()
    barrier = pltpu.get_barrier_semaphore()

    def wrap(i, size):
        return jnp.where(i >= size, i - size, i)

    greeted = [{"pencil": wrap(me + i, PENCILS)} for i in range(1, PENCILS)]
    greeted += [{"dp": wrap(group + i, GROUPS)} for i in range(1, GROUPS)]
    for to in greeted:
        pl.semaphore_signal(barrier, inc=1, device_id=to, device_id_type=MESH)
    for part in range(1, 4):
        load(field_hbm, field, part, 4 * part).start()
    for copy in copies[4:]:
        copy.start()
    for part in range(4):
        load(cot_hbm, cot, 4 + part, 4 * part).start()

    def send(turn, half):
        for dy, dz in FARTHEST:
            to = wrap(row + dy * 8, PENCILS) + wrap(spot + dz, 8)
            pltpu.make_async_remote_copy(
                src_ref=sbuf.at[turn, half, to],
                dst_ref=rbuf.at[turn, half, me],
                send_sem=ssem.at[turn, half],
                recv_sem=rsem.at[turn, half],
                device_id={"pencil": to},
                device_id_type=MESH,
            ).start()
        rbuf[turn, half, me] = sbuf[turn, half, me]

    def whole(turn, half):
        return pltpu.make_async_remote_copy(
            src_ref=sbuf.at[turn, half, pl.ds(0, PENCILS - 1)],
            dst_ref=rbuf.at[turn, half, pl.ds(0, PENCILS - 1)],
            send_sem=ssem.at[turn, half],
            recv_sem=rsem.at[turn, half],
            device_id={"pencil": lax.rem(me + 1, PENCILS)},
            device_id_type=MESH,
        )

    def analyse(source, x, x_half):
        pair = jnp.concatenate([source[x], source[x + 1]], axis=1)
        rows = dot(second_t[...], pair)
        analysed[pl.ds(x_half, 2 * MY, stride=HALF), :] = rows[:, :FEATS]
        analysed[pl.ds(x_half + 1, 2 * MY, stride=HALF), :] = rows[:, FEATS:]
        return rows

    def pack(turn, half):
        sbuf[turn, half] = analysed[...].astype(BF16).reshape(PENCILS, MESSAGE, FEATS)

    def gather_modes(turn):
        total = None
        for half in range(2):
            whole(turn, half).wait_recv()
            term = dot(first[:, BLOCK * half : BLOCK * (half + 1)], rbuf[turn, half].reshape(BLOCK, FEATS))
            total = term if total is None else total + term
        return total

    def scatter_modes(turn, modes):
        narrow = modes.astype(BF16)
        for half in range(2):
            rows = dot(first_t[BLOCK * half : BLOCK * (half + 1), : 2 * MX], narrow)
            sbuf[turn, half] = rows.astype(BF16).reshape(PENCILS, MESSAGE, FEATS)
            send(turn, half)

    def unpack(turn, half):
        whole(turn, half).wait_recv()
        scratch[...] = rbuf[turn, half].astype(F32).reshape(BLOCK, FEATS)

    rows128, lanes128 = iotas((FEATS, FEATS))
    same = rows128 // C == lanes128 // C
    in_keep = (rows128 % 64) // RANK == lanes128 // C

    def field_rows():
        for copy in copies[:4]:
            copy.wait()
        for half in range(2):
            for part in range(2):
                load(field_hbm, field, 2 * half + part, HALF * half + 4 * part).wait()
                for x in range(4 * part, 4 * part + 4, 2):
                    analyse(field, HALF * half + x, x)
            pack(0, half)
        pl.semaphore_wait(barrier, len(greeted))
        for half in range(2):
            send(0, half)

    def weights():
        for copy in copies[4:]:
            copy.wait()
        joined = dot_tn(first_core[...], second_core[...], HIGHEST)
        joined2 = jnp.concatenate([joined, joined], axis=0)
        spread = select((RANK, 1024), lambda r, l: r == 2 * (l // 128) + (l % 128) // 64)
        joined_wide[...] = dot(joined2, spread, HIGHEST)
        to_lanes = select((C, FEATS), lambda r, l: r == l % C, BF16)
        to_rows = select((FEATS, C), lambda r, l: r % C == l, BF16)
        pair_rows = select((FEATS, RANK), lambda r, l: r % RANK == l, BF16)
        for beta in range(RANK // 2):
            rows = output_core[2 * RANK * beta : 2 * RANK * beta + 2 * RANK].astype(BF16)
            low, high = rows[:RANK], rows[RANK:]
            tall = jnp.concatenate([low] * PLANES + [high] * PLANES, axis=0)
            wide = jnp.where(in_keep, dot(tall, to_lanes), 0.0)
            out_wide[128 * beta : 128 * beta + 128, :] = wide.astype(BF16)
        in_rows = dot(pair_rows, input_core[...].astype(BF16)).astype(BF16)
        in_wide[...] = jnp.where(in_keep, dot(in_rows, to_lanes), 0.0).astype(BF16)
        mix_rows = dot(to_rows, mix[...]).astype(BF16)
        mix_wide[...] = jnp.where(same, dot(mix_rows, to_lanes), 0.0).astype(BF16)
        mix_rows = dot_nt(to_rows, mix[...]).astype(BF16)
        mix_wide_t[...] = jnp.where(same, dot(mix_rows, to_lanes), 0.0).astype(BF16)
        wide_bias = dot(bias[...], to_lanes.astype(F32), HIGHEST)
        rows64, _ = iotas((2 * MY, FEATS))
        terms = jnp.zeros((2 * MY, FEATS), F32)
        for i in range(3):
            term = wide_bias.astype(BF16).astype(F32)
            terms = jnp.where(rows64 == i, term, terms)
            wide_bias = wide_bias - term
        bias_rows[...] = terms.astype(BF16)
        for part in range(4):
            load(cot_hbm, cot, 4 + part, 4 * part).wait()

    def mix_forward():
        modes = gather_modes(0)
        spectrum[...] = modes
        doubled = dot_nt(modes.astype(BF16), in_wide[...])
        narrow2[...] = doubled
        for beta in range(RANK // 2):
            cols = slice(128 * beta, 128 * beta + 128)
            zed[:, cols] = (joined_wide[:, cols] * doubled).astype(BF16)
        scatter_modes(1, dot(zed[...], out_wide[...]))

    def activate(x, rows_x):
        rhs = jnp.concatenate([mix_wide[...], rows_x, bias_rows[...]], axis=0)
        for y in range(0, NY, 128):
            lhs = jnp.concatenate([field[x, y : y + 128], second[y : y + 128]], axis=1)
            combined = dot(lhs, rhs)
            cumulative = 0.5 + 0.5 * lax.erf(combined * math.sqrt(0.5))
            density = jnp.exp2(combined * combined * (-0.5 * math.log2(math.e))) * (1.0 / math.sqrt(2.0 * math.pi))
            act[x, y : y + 128] = (combined * cumulative).astype(BF16)
            derivative = cumulative + combined * density
            up[x, y : y + 128] = (cot[x, y : y + 128].astype(F32) * derivative).astype(BF16)

    def sweep(base, step):
        def body(j, carry):
            for i in range(4):
                x = 4 * j + i
                step(base + x, scratch[pl.ds(x, 2 * MY, stride=HALF), :].astype(BF16))
            return carry

        lax.fori_loop(0, HALF // 4, body, 0)

    def activation():
        total = jnp.zeros((1, FEATS), F32)
        for half in range(2):
            unpack(1, half)
            base = HALF * half

            def after(j, carry, base=base):
                rows = analyse(up, base + 2 * j, 2 * j)
                return carry + rows[0:1, :FEATS] + rows[0:1, FEATS:]

            sweep(base, activate)
            for j in range(HALF // 2):
                total = after(j, total)
            pack(2, half)
            send(2, half)
        rows_sum[...] = total

    def mix_gradient():
        products[...] = jnp.zeros_like(products)

        def accumulate(x, carry):
            products[...] += dot_tn(field[x], up[x])
            return carry

        lax.fori_loop(0, ROWS, accumulate, 0)

    def mix_backward():
        upstream = gather_modes(2)
        upstream_b = upstream.astype(BF16)
        dz = dot_nt(upstream_b, out_wide[...])
        dn = joined_wide[:, 0:128] * dz[:, 0:128]
        for beta in range(1, RANK // 2):
            cols = slice(128 * beta, 128 * beta + 128)
            dn = dn + joined_wide[:, cols] * dz[:, cols]
        return upstream_b, dz, dn.astype(BF16)

    def send_returned(upstream_b, dz, dn_b):
        scatter_modes(3, dot(dn_b, in_wide[...]))

    def fold_tables():
        fold_rank[...] = select(
            (1024, FEATS), lambda r, l: l % RANK == 2 * (r // 128) + (r % 128) // 64, BF16
        )
        fold_lanes[...] = select(
            (4 * FEATS, FEATS), lambda r, l: r % C + 32 * (r // FEATS) == l, BF16
        )
        mixed = jnp.where(same, products[...], 0.0) * (MIX_SCALE / CORE_SCALE)
        mixed = (mixed[0:32] + mixed[32:64]) + (mixed[64:96] + mixed[96:128])
        unit = float(np.asarray(1.0 / math.sqrt(NY), dtype=np.float32).astype(jnp.bfloat16))
        biases = rows_sum[...] * (MIX_SCALE / CORE_SCALE / unit)
        fold = select((FEATS, FEATS), lambda r, l: r % C == l)
        fold_bias = select((FEATS, FEATS), lambda r, l: r % C + 64 == l)
        misc[...] = dot(mixed, fold, HIGHEST) + dot(biases, fold_bias, HIGHEST)

    def core_gradients(upstream_b, dz, dn_b):
        product = jnp.concatenate(
            [dz[:, 128 * b : 128 * b + 128] * narrow2[...] for b in range(RANK // 2)], axis=1
        ).astype(BF16)
        djoined = dot(product, fold_rank[...])
        djoined = (djoined[:MX] + djoined[MX:]).astype(BF16)
        first_part = dot_nt(second_core[...].astype(BF16), djoined[:, :RANK])
        second_part = dot(first_core[...].astype(BF16), djoined)
        rows16, lanes16 = iotas((RANK, FEATS))
        second_part = jnp.where(rows16 % 8 == lanes16 // RANK, second_part, 0.0)
        second_part = jnp.concatenate(
            [jnp.sum(second_part[8 * i : 8 * i + 8], axis=0, keepdims=True) for i in range(2)], axis=0
        )
        rows = []
        for beta in range(RANK // 2):
            outer = dot_tn(zed[:, 128 * beta : 128 * beta + 128], upstream_b)
            outer = jnp.where(in_keep, outer, 0.0)
            for base in (0, 64):
                rows.append(
                    (outer[base : base + 16] + outer[base + 16 : base + 32])
                    + (outer[base + 32 : base + 48] + outer[base + 48 : base + 64])
                )
        wide = jnp.concatenate(
            [jnp.concatenate(rows[4 * q : 4 * q + 4], axis=0) for q in range(4)], axis=1
        )
        packed = dot(wide.astype(BF16), fold_lanes[...])
        inner = jnp.where(in_keep, dot_tn(dn_b, spectrum[...].astype(BF16)), 0.0)
        inner = sum(inner[RANK * i : RANK * (i + 1)] for i in range(1, 2 * PLANES)) + inner[0:RANK]
        inner = misc[0:RANK] + dot(inner.astype(BF16), fold_lanes[FEATS : 2 * FEATS])
        rest[...] = misc[...]
        rest[0:RANK] = inner
        rest[RANK:C, 32:64] = first_part
        for q in range(GROUPS):
            parts = [packed[8 * q : 8 * q + 8], rest[4 * q : 4 * q + 4], second_part, jnp.zeros((2, FEATS), F32)]
            gsend[q] = jnp.concatenate(parts, axis=0).astype(BF16)

    def to_groups(source, target, sent, received):
        def start(i, carry):
            to = wrap(group + i, GROUPS)
            pltpu.make_async_remote_copy(
                src_ref=source(to), dst_ref=target.at[group], send_sem=sent, recv_sem=received,
                device_id={"dp": to}, device_id_type=MESH,
            ).start()
            return carry

        lax.fori_loop(1, GROUPS, start, 0, unroll=True)

    def wait_for(target, count, sent, received):
        others = target.at[pl.ds(0, count)]
        return pltpu.make_async_remote_copy(
            src_ref=others, dst_ref=others, send_sem=sent, recv_sem=received,
            device_id={"pencil": lax.rem(me + 1, PENCILS)}, device_id_type=MESH,
        )

    all_groups = wait_for(grecv, GROUPS - 1, gssem, grsem)
    all_pencils = wait_for(brecv, PENCILS - 1, bssem, brsem)
    all_last = wait_for(grads_out, GROUPS - 1, cssem, crsem)

    def sum_groups_send():
        to_groups(lambda to: gsend.at[to], grecv, gssem, grsem)
        grecv[group] = gsend[group]

    def sum_groups():
        all_groups.wait_recv()
        chunk = grecv[0].astype(F32)
        for q in range(1, GROUPS):
            chunk = chunk + grecv[q].astype(F32)
        second_out[...] = chunk * CORE_SCALE
        bsend[...] = chunk.astype(BF16)

        def start(i, carry):
            pltpu.make_async_remote_copy(
                src_ref=bsend, dst_ref=brecv.at[me], send_sem=bssem, recv_sem=brsem,
                device_id={"pencil": wrap(me + 1 + i, PENCILS)}, device_id_type=MESH,
            ).start()
            return carry

        lax.fori_loop(0, PENCILS - 1, start, 0, unroll=4)
        brecv[me] = bsend[...]

    def sum_pencils():
        all_pencils.wait_recv()
        total = brecv[0].astype(F32)
        for q in range(1, PENCILS):
            total = total + brecv[q].astype(F32)
        total = total * CORE_SCALE
        csend[...] = total
        to_groups(lambda to: csend, grads_out, cssem, crsem)
        grads_out[group] = total

    def last():
        all_last.wait_recv()

    def finish(x, rows_x):
        rhs = jnp.concatenate([mix_wide_t[...], rows_x], axis=0)
        for y in range(0, NY, 128):
            lhs = jnp.concatenate([up[x, y : y + 128], second[y : y + 128, : 2 * MY]], axis=1)
            adjoint[x, y : y + 128] = dot(lhs, rhs).astype(BF16)

    def finish_half(half):
        unpack(3, half)
        sweep(HALF * half, finish)

    state = {}
    steps = [
        field_rows, weights, mix_forward, activation, mix_gradient, fold_tables,
        lambda: state.update(modes=mix_backward()),
        lambda: core_gradients(*state["modes"]),
        sum_groups_send, lambda: send_returned(*state["modes"]),
        sum_groups, lambda: finish_half(0), sum_pencils, lambda: finish_half(1), last,
    ]
    for step in steps:
        step()

    for copy in (all_groups, all_pencils, all_last):
        copy.wait_send()
    for turn in range(4):
        for half in range(2):
            whole(turn, half).wait_send()


def write_out(
    act, adjoint, grads, second_in,
    act_hbm, adjoint_hbm, first_hbm, second_hbm, output_hbm, input_hbm, mix_hbm, bias_hbm,
    first, second, output, inner, mix, bias, packed, misc, sem,
):
    large = []
    for i in range(4):
        part = pl.ds(ROWS // 4 * i, ROWS // 4)
        large.append(pltpu.make_async_copy(act.at[part], act_hbm.at[part], sem.at[6 + i]))
        large.append(pltpu.make_async_copy(adjoint.at[part], adjoint_hbm.at[part], sem.at[10 + i]))
    for copy in large:
        copy.start()
    for i in range(RANK):
        second[i : i + 1] = second_in[12 + i // 8 : 13 + i // 8, RANK * (i % 8) : RANK * (i % 8) + RANK]
    for q in range(GROUPS):
        packed[8 * q : 8 * q + 8] = grads[q, 0:8]
        misc[4 * q : 4 * q + 4] = grads[q, 8:12]
    for quarter in range(4):
        output[64 * quarter : 64 * quarter + 64] = packed[:, 32 * quarter : 32 * quarter + 32]
    mix[...] = misc[:, 0:32]
    inner[...] = misc[0:RANK, 32:64]
    first[...] = misc[RANK:C, 32:64]
    bias[...] = misc[0:1, 64:96]
    pairs = [
        (first, first_hbm), (second, second_hbm), (output, output_hbm),
        (inner, input_hbm), (mix, mix_hbm), (bias, bias_hbm),
    ]
    small = [pltpu.make_async_copy(a, b, sem.at[i]) for i, (a, b) in enumerate(pairs)]
    for copy in small:
        copy.start()
    for copy in large + small:
        copy.wait()


def shards(field, cotangent, first_core, second_core, output_core, input_core, channel_mix, channel_bias):
    slab = (ROWS, NY, FEATS)
    vmem = pl.BlockSpec(memory_space=pltpu.VMEM)
    hbm = pl.BlockSpec(memory_space=pltpu.HBM)
    dma = pltpu.SemaphoreType.DMA
    smalls = [(RANK, MX), (RANK, RANK), (RANK * RANK, C), (RANK, C), (C, C), (1, C)]
    types = [F32, F32, F32, F32, BF16, F32]
    act, adjoint, grads, second_total = pl.pallas_call(
        kernel,
        out_shape=[
            jax.ShapeDtypeStruct(slab, BF16),
            jax.ShapeDtypeStruct(slab, BF16),
            jax.ShapeDtypeStruct((GROUPS, CHUNK, FEATS), F32),
            jax.ShapeDtypeStruct((16, FEATS), F32),
        ],
        in_specs=[hbm] * 9,
        out_specs=[vmem] * 4,
        scratch_shapes=[
            pltpu.VMEM(slab, BF16),
            pltpu.VMEM(slab, BF16),
            pltpu.VMEM(slab, BF16),
            pltpu.VMEM((BLOCK, FEATS), F32),
            pltpu.VMEM((BLOCK, FEATS), F32),
            pltpu.VMEM((4, 2, PENCILS, MESSAGE, FEATS), BF16),
            pltpu.VMEM((4, 2, PENCILS, MESSAGE, FEATS), BF16),
        ]
        + [pltpu.VMEM(s, t) for s, t in zip(smalls, types)]
        + [
            pltpu.VMEM((2 * MY, NY), BF16),
            pltpu.VMEM((2 * MX, 2 * NX), BF16),
            pltpu.VMEM((NY, FEATS), BF16),
            pltpu.VMEM((2 * NX, FEATS), BF16),
            pltpu.VMEM((2 * MX, 1024), F32),
            pltpu.VMEM((1024, FEATS), BF16),
            pltpu.VMEM((FEATS, FEATS), BF16),
            pltpu.VMEM((FEATS, FEATS), BF16),
            pltpu.VMEM((FEATS, FEATS), BF16),
            pltpu.VMEM((2 * MY, FEATS), BF16),
            pltpu.VMEM((2 * MX, FEATS), F32),
            pltpu.VMEM((2 * MX, 1024), BF16),
            pltpu.VMEM((2 * MX, FEATS), F32),
            pltpu.VMEM((FEATS, FEATS), F32),
            pltpu.VMEM((1, FEATS), F32),
            pltpu.VMEM((1024, FEATS), BF16),
            pltpu.VMEM((4 * FEATS, FEATS), BF16),
            pltpu.VMEM((C, FEATS), F32),
            pltpu.VMEM((C, FEATS), F32),
            pltpu.VMEM((GROUPS, CHUNK, FEATS), BF16),
            pltpu.VMEM((GROUPS, CHUNK, FEATS), BF16),
            pltpu.VMEM((CHUNK, FEATS), BF16),
            pltpu.VMEM((PENCILS, CHUNK, FEATS), BF16),
            pltpu.VMEM((CHUNK, FEATS), F32),
            dma((8,)),
            dma((20,)),
            dma((4, 2)),
            dma((4, 2)),
            dma,
            dma,
            dma,
            dma,
            dma,
            dma,
        ],
        compiler_params=pltpu.CompilerParams(
            collective_id=0, has_side_effects=True, vmem_limit_bytes=40 * 2**20
        ),
    )(
        *[
            pltpu.with_memory_space_constraint(a, pltpu.HBM)
            for a in (
                field[0],
                cotangent[0],
                first_core.T,
                second_core[:, 0, :],
                output_core.transpose(0, 2, 1).reshape(RANK * RANK, C),
                input_core,
                channel_mix,
                channel_bias[None],
                jnp.asarray(tables()),
            )
        ]
    )
    results = pl.pallas_call(
        write_out,
        out_shape=[jax.ShapeDtypeStruct(slab, BF16), jax.ShapeDtypeStruct(slab, BF16)]
        + [jax.ShapeDtypeStruct(s, F32) for s in smalls],
        in_specs=[vmem] * 4,
        out_specs=[hbm] * 8,
        scratch_shapes=[pltpu.VMEM(s, F32) for s in smalls + [(64, FEATS), (C, FEATS)]] + [dma((14,))],
        compiler_params=pltpu.CompilerParams(vmem_limit_bytes=16 * 2**20),
    )(act, adjoint, grads, second_total)
    act, adjoint, first, second, output, inner, mix, bias = results
    return (
        act[None],
        adjoint[None],
        first.T,
        second[:, None, :],
        output.reshape(RANK, RANK, C).transpose(0, 2, 1),
        inner,
        mix,
        bias[0],
    )


def solution(mesh):
    slabs = P("dp", "pencil", None, None)
    column = P(None, "pencil", None)
    return jax.shard_map(
        shards,
        mesh=mesh,
        in_specs=(slabs, slabs, P(), column, P(), P(), P(), P()),
        out_specs=(slabs, slabs, P(), column, P(), P(), P(), P()),
        check_vma=False,
    )
```
